256 devices in a mesh: tile: 16 (over x, y), frame: 16 (over z, core).
Axes of the slice: x: 4, y: 4, z: 8, core: 2. Of those that a mesh axis runs over, the one named last changes fastest.
Arguments:
- object_field: float32 [2, 4096, 4096], P(None, 'tile', 'frame'), may hold values from -4 to 4
- probe_modes: float32 [2, 3, 256, 256], replicated, may hold values from -4 to 4
- measured: float32 [256, 256, 256], P(('tile', 'frame')), may hold values from 0.2 to 2.5
- offsets: int32 [256, 2], P(('tile', 'frame')), may hold values from 0 to 255
- ramp_steps: int32 [256, 2], P(('tile', 'frame')), may hold values from 0 to 7
Outputs:
- object_final: float32 [2, 4096, 4096], P(None, 'tile', 'frame')
- probe_final: float32 [2, 3, 256, 256], replicated
- position_grad: float32 [256, 2], P(('tile', 'frame'))
The draws below stay inside these ranges and needn't reach their ends.
All inputs are finite; a program needn't handle non-finite values.
Results may differ from the reference program's by a relative error of at most 0.0003.
Values sent between devices are 32-bit elements; how exact they have to be, the bound alone decides.
No kernel may reach another device: no remote copies, remote signals or barrier semaphores. Data moves between devices by JAX's collectives and lax.ppermute only.
A program may use at most 128 MiB of HBM per device.

```python
import math
import jax
import jax.numpy as jnp
from jax import lax

DET = 256
MODES = 3
TILE = 256
FRAME_DEV = 1
RAMPS = 8
ITERS = 2
FRAMES = 256
OBJ_ROWS = 4096
OBJ_COLS = 4096
N_TILE = 16
N_FRAME = 16


def with_ends(values, rng, smallest, top_value):
    longest = values.shape.index(max(values.shape))
    spots = []
    for shift in (0, 1):
        where = [jax.random.randint(jax.random.fold_in(rng, axis), (), 0, length) for axis, length in enumerate(values.shape)]
        where[longest] = (where[longest] + shift) % values.shape[longest]
        spots.append(tuple(where))
    return values.at[spots[0]].set(smallest).at[spots[1]].set(top_value)


def block_scale(rng, shape, shards, smallest, largest):
    def one(axis_at, blocks):
        heights = jax.random.uniform(jax.random.fold_in(jax.random.fold_in(rng, 6), axis_at), (blocks,), jnp.float32, smallest / len(shards), largest / len(shards))
        return jnp.repeat(jnp.exp(heights), shape[axis_at] // blocks).reshape((-1,) + (1,) * (len(shape) - axis_at - 1))

    loudness = one(*shards[0])
    for cut in shards[1:]:
        loudness = loudness * one(*cut)
    return loudness


def centred(rng, shape, scale, most, cuts=(), held_as=jnp.bfloat16):
    entries = scale * jax.random.normal(rng, shape, jnp.float32)
    if cuts:
        entries = entries * block_scale(rng, shape, cuts, -0.22, 0.18)
    return jnp.clip(entries, -most, most).astype(held_as)


def setup_inputs(seed: int = 0) -> dict:
    seeds = jax.random.split(jax.random.key(seed), 6)
    return {
        "object_field": centred(seeds[0], (2, OBJ_ROWS, OBJ_COLS), 0.7, 4.0, ((1, 16), (2, 16)), jnp.float32),
        "probe_modes": centred(seeds[1], (2, MODES, DET, DET), 0.6, 4.0, (), jnp.float32),
        "measured": jnp.clip(0.2 + 2.3 * jax.random.uniform(seeds[2], (FRAMES, DET, DET), jnp.float32) ** block_scale(seeds[2], (FRAMES, DET, DET), ((0, 256),), -0.2, 0.2), 0.2, 2.5),
        "offsets": with_ends(jax.random.randint(seeds[3], (FRAMES, 2), 0, TILE), jax.random.fold_in(seeds[3], 1), 0, TILE - 1).astype(jnp.int32),
        "ramp_steps": with_ends(jax.random.randint(seeds[4], (FRAMES, 2), 0, RAMPS), jax.random.fold_in(seeds[4], 1), 0, RAMPS - 1).astype(jnp.int32),
    }


object_step = 0.05
probe_step = 0.5
fresnel = 0.25

def dft_tables(length):
    counter = jnp.arange(length, dtype=jnp.int32)
    product = counter[:, None] * counter[None, :] % length
    angles = 2.0 * math.pi / length * product.astype(jnp.float32)
    scaling = 1.0 / math.sqrt(length)
    return (jnp.cos(angles) * scaling, -jnp.sin(angles) * scaling)

def transform(real_part, imag_part, cos_table, sin_table):
    highest = lax.Precision.HIGHEST
    left_real = jnp.einsum('jk,mkl->mjl', cos_table, real_part, precision=highest) - jnp.einsum('jk,mkl->mjl', sin_table, imag_part, precision=highest)
    left_imag = jnp.einsum('jk,mkl->mjl', cos_table, imag_part, precision=highest) + jnp.einsum('jk,mkl->mjl', sin_table, real_part, precision=highest)
    out_real = jnp.einsum('mjl,lk->mjk', left_real, cos_table, precision=highest) - jnp.einsum('mjl,lk->mjk', left_imag, sin_table, precision=highest)
    out_imag = jnp.einsum('mjl,lk->mjk', left_real, sin_table, precision=highest) + jnp.einsum('mjl,lk->mjk', left_imag, cos_table, precision=highest)
    return (out_real, out_imag)

def frame_loss(patch_area, modes_in, shift_amount, target):
    length = patch_area.shape[-1]
    cos_table, sin_table = dft_tables(length)
    exit_real = modes_in[0] * patch_area[0] - modes_in[1] * patch_area[1]
    exit_imag = modes_in[0] * patch_area[1] + modes_in[1] * patch_area[0]
    spec_real, spec_imag = transform(exit_real, exit_imag, cos_table, sin_table)
    counter = jnp.arange(length, dtype=jnp.int32)
    signed = jnp.where(counter < length // 2, counter, counter - length).astype(jnp.float32)
    chirp_phase = -math.pi * fresnel / length * signed * signed
    phase_rows = chirp_phase - 2.0 * math.pi / length * signed * shift_amount[0]
    phase_cols = chirp_phase - 2.0 * math.pi / length * signed * shift_amount[1]
    phases = phase_rows[:, None] + phase_cols[None, :]
    kernel_real = jnp.cos(phases)
    kernel_imag = jnp.sin(phases)
    prop_real = kernel_real * spec_real - kernel_imag * spec_imag
    prop_imag = kernel_real * spec_imag + kernel_imag * spec_real
    wave_real, wave_imag = transform(prop_real, prop_imag, cos_table, -sin_table)
    intensity = lax.optimization_barrier(jnp.sum(wave_real * wave_real + wave_imag * wave_imag, axis=0))
    misfit = intensity - target
    return 0.5 * jnp.sum(misfit * misfit)

def frame_gradients(window, modes_in, measured, corners, ramp_steps):
    det_size = modes_in.shape[-1]

    def visit_frame(running, inputs):
        grad_window, grad_modes = running
        corner, ramp_index, target = inputs
        anchor = (jnp.int32(0), corner[0], corner[1])
        patch_area = lax.dynamic_slice(window, anchor, (2, det_size, det_size))
        shift_amount = ramp_index.astype(jnp.float32) / RAMPS

        def local_loss(patch_in, probe_in, shift_in):
            return frame_loss(patch_in, probe_in, shift_in, target)
        result, pullback = jax.vjp(local_loss, patch_area, modes_in, shift_amount)
        grad_patch, grad_probe, grad_shift = pullback(jnp.ones_like(result))
        current = lax.dynamic_slice(grad_window, anchor, (2, det_size, det_size))
        grad_window = lax.dynamic_update_slice(grad_window, current + grad_patch, anchor)
        return ((grad_window, grad_modes + grad_probe), grad_shift)
    initial = (jnp.zeros_like(window), jnp.zeros_like(modes_in))
    (grad_window, grad_modes), grad_shift = lax.scan(visit_frame, initial, (corners, ramp_steps, measured))
    return (grad_window, grad_modes, grad_shift)

def reference(object_field, probe_modes, measured, offsets, ramp_steps):
    rows_total = TILE * N_TILE
    cols_total = TILE * N_FRAME
    padded = jnp.pad(object_field, ((0, 0), (0, TILE), (0, TILE)))
    frame_index = jnp.arange(FRAMES, dtype=jnp.int32)
    device = frame_index // FRAME_DEV
    row_start = device // N_FRAME * TILE + offsets[:, 0]
    col_start = device % N_FRAME * TILE + offsets[:, 1]
    corners = jnp.stack([row_start, col_start], axis=1).astype(jnp.int32)
    modes_now = probe_modes
    grad_shift = jnp.zeros((FRAMES, 2), jnp.float32)
    for iteration in range(ITERS):
        grad_padded, grad_modes, grad_shift = frame_gradients(padded, modes_now, measured, corners, ramp_steps)
        current_object = padded[:, :rows_total, :cols_total] - object_step * grad_padded[:, :rows_total, :cols_total]
        padded = jnp.pad(current_object, ((0, 0), (0, TILE), (0, TILE)))
        modes_now = modes_now - probe_step / FRAMES * grad_modes
    return (padded[:, :rows_total, :cols_total], modes_now, grad_shift / DET)
```

```python
import math

import jax
import jax.numpy as jnp
import numpy as np
from jax import lax
from jax.experimental import pallas as pl
from jax.experimental.pallas import tpu as pltpu
from jax.sharding import PartitionSpec as P

DET = 256
HALF = 128
MODES = 3
RAMPS = 8
STRIP = 16

object_step = 0.05
probe_step = 0.5
fresnel = 0.25

F32 = jnp.float32
BF16 = jnp.bfloat16


def circulant_blocks(eigenvalues):
    counter = np.arange(DET)
    waves = np.exp(2j * np.pi * (np.outer(counter, counter) % DET) / DET)
    column = waves @ eigenvalues / DET
    full = column[(counter[:, None] - counter[None, :]) % DET]
    first, second = full[:HALF, :HALF], full[:HALF, HALF:]

    def real_form(block):
        return np.block([[block.real, -block.imag], [block.imag, block.real]])

    return np.stack([real_form((first + second) / 2), real_form((first - second) / 2)])


def split_table(table):
    table = table.astype(np.float32)
    high = table.astype(BF16)
    low = (table - high.astype(np.float32)).astype(BF16)
    return np.stack([high, low], axis=-3)


def shift_tables():
    counter = np.arange(DET)
    signed = np.where(counter < DET // 2, counter, counter - DET).astype(np.float64)
    chirp = -np.pi * fresnel * signed * signed / DET
    slope = -2j * np.pi * signed / DET
    plain, derived = [], []
    for step in range(RAMPS):
        factor = np.exp(1j * chirp + slope * (step / RAMPS))
        plain.append(circulant_blocks(factor))
        derived.append(circulant_blocks(slope * factor))
    plain, derived = np.stack(plain), np.stack(derived)
    slope_blocks = circulant_blocks(slope)
    turned = np.swapaxes(plain, -1, -2)
    return (
        split_table(plain),
        split_table(turned),
        split_table(derived),
        split_table(np.swapaxes(slope_blocks, -1, -2)),
    )


def split(value):
    high = value.astype(BF16)
    return high, (value - high.astype(F32)).astype(BF16)


def product(left, right):
    return lax.dot_general(
        left, right, (((1,), (0,)), ((), ())), preferred_element_type=F32
    )


def gradient_kernel(last, rate, *refs):
    refs = list(refs)
    take = lambda count: [refs.pop(0) for _ in range(count)]
    (scalars,) = take(1)
    if last:
        patch_in, merged, from_above, from_below, grad_before = take(5)
        total_mine, total_other = take(2)
    else:
        own, right, lower = take(3)
    probe, measured = take(2)
    plain0, turned0, plain1, turned1 = take(4)
    if last:
        derived0, slope1 = take(2)
    if last:
        grad_out, probe_out, keep_out, send_out, shift_out = take(5)
    else:
        grad_out, patch_out, keep_out, send_out = take(4)
    doubled, field, high, low, result, z_high, z_low, z_result = take(8)
    if last:
        slope_result, derived_result = take(2)

    row0, col0, core = scalars[0], scalars[1], scalars[2]

    def build(step, _):
        start = pl.multiple_of(step * STRIP, STRIP)
        rows = pl.ds(start, STRIP)
        again = pl.ds(start + DET, STRIP)
        row_at = lax.broadcasted_iota(jnp.int32, (STRIP, DET), 0) + start
        col_at = lax.broadcasted_iota(jnp.int32, (STRIP, DET), 1)
        if last:
            outside = ((row_at < row0) & (scalars[3] == 1)) | ((col_at < col0) & (scalars[4] == 1))
        for part in range(2):
            if last:
                moved = jnp.where(row_at >= row0, from_above[part, rows, :], from_below[part, rows, :])
                cells = patch_in[part, rows, :] - object_step * (merged[part, rows, :] + moved)
                cells = jnp.where(outside, 0.0, cells)
            else:
                cells = jnp.where(
                    row_at >= row0,
                    jnp.where(col_at >= col0, own[part, rows, :], right[part, rows, :]),
                    lower[part, rows, :],
                )
                patch_out[part, rows, :] = cells
            doubled[part, rows, :] = cells
            doubled[part, again, :] = cells
        if last:
            for mode in range(MODES):
                mine = total_mine[mode, rows, :]
                other = total_other[mode, rows, :]
                probe_out[0, mode, rows, :] = probe[0, mode, rows, :] - rate * jnp.where(core == 0, mine, other)
                probe_out[1, mode, rows, :] = probe[1, mode, rows, :] - rate * jnp.where(core == 0, other, mine)
        return 0

    lax.fori_loop(0, DET // STRIP, build, 0)
    modes = probe_out if last else probe
    back = lax.rem(DET - col0, DET)

    def rows_from(part, first):
        down = lax.rem(first, 8)
        at = pl.ds(pl.multiple_of(first - down, 8), STRIP + 8)
        return pltpu.roll(doubled[part, at, :], lax.rem(STRIP + 8 - down, STRIP + 8), 0)[:STRIP]

    def enter(step, _):
        start = pl.multiple_of(step * STRIP, STRIP)
        rows = pl.ds(start, STRIP)
        real = pltpu.roll(rows_from(0, row0 + start), back, 1)
        imag = pltpu.roll(rows_from(1, row0 + start), back, 1)
        field[0, rows, :] = real
        field[1, rows, :] = imag
        for mode in range(MODES):
            probe_real = modes[0, mode, rows, :]
            probe_imag = modes[1, mode, rows, :]
            exit_real = probe_real * real - probe_imag * imag
            exit_imag = probe_real * imag + probe_imag * real
            at = pl.ds(pl.multiple_of(mode * DET + start, STRIP), STRIP)
            for block, sign in ((0, 1.0), (1, -1.0)):
                both = jnp.concatenate(
                    [
                        exit_real[:, :HALF] + sign * exit_real[:, HALF:],
                        exit_imag[:, :HALF] + sign * exit_imag[:, HALF:],
                    ],
                    axis=1,
                )
                high[block, at, :], low[block, at, :] = split(both)
        return 0

    lax.fori_loop(0, DET // STRIP, enter, 0)

    def times_right(block, mode, table, where):
        at = pl.ds(mode * DET, DET)
        left_high, left_low = high[block, at, :], low[block, at, :]
        where[block, at, :] = (
            product(left_high, table[block, 0])
            + product(left_low, table[block, 0])
            + product(left_high, table[block, 1])
        )

    def times_left(block, mode, table, where):
        at = pl.ds(mode * DET, DET)
        right_high, right_low = z_high[block, :, at], z_low[block, :, at]
        where[block, :, at] = (
            product(table[block, 0], right_high)
            + product(table[block, 0], right_low)
            + product(table[block, 1], right_high)
        )

    for block in range(2):
        for mode in range(MODES):
            times_right(block, mode, turned1, result)
            if last:
                times_right(block, mode, slope1, slope_result)

    def rows_to_blocks(step, _):
        start = pl.multiple_of(step * STRIP, STRIP)
        for mode in range(MODES):
            top = pl.ds(pl.multiple_of(mode * DET + start, STRIP), STRIP)
            bottom = pl.ds(pl.multiple_of(mode * DET + HALF + start, STRIP), STRIP)
            sums = [(result[col, top, :] + result[col, bottom, :]) for col in range(2)]
            gaps = [(result[col, top, :] - result[col, bottom, :]) for col in range(2)]
            for block, pair in ((0, sums), (1, gaps)):
                for part in range(2):
                    lanes = slice(part * HALF, (part + 1) * HALF)
                    both = jnp.concatenate([pair[0][:, lanes], pair[1][:, lanes]], axis=1)
                    at = pl.ds(pl.multiple_of(part * HALF + start, STRIP), STRIP)
                    cols = pl.ds(mode * DET, DET)
                    z_high[block, at, cols], z_low[block, at, cols] = split(both)
        return 0

    lax.fori_loop(0, HALF // STRIP, rows_to_blocks, 0)

    for block in range(2):
        for mode in range(MODES):
            times_left(block, mode, plain0, z_result)
            if last:
                times_left(block, mode, derived0, derived_result)

    def misfits(step, running):
        start = pl.multiple_of(step * STRIP, STRIP)
        low_rows = pl.ds(start, STRIP)
        high_rows = pl.ds(pl.multiple_of(start + HALF, STRIP), STRIP)

        def waves(mode, part):
            at = pl.ds(pl.multiple_of(part * HALF + start, STRIP), STRIP)
            cols = pl.ds(mode * DET, DET)
            even, odd = z_result[0, at, cols], z_result[1, at, cols]

            def spread(value):
                return jnp.concatenate(
                    [value[:, :HALF] + value[:, HALF:], value[:, :HALF] - value[:, HALF:]], axis=1
                )

            return spread(even + odd), spread(even - odd)

        top_sum = bottom_sum = None
        held = []
        for mode in range(MODES):
            for part in range(2):
                top, bottom = waves(mode, part)
                held.append((mode, part, top, bottom))
                top_sum = top * top if top_sum is None else top_sum + top * top
                bottom_sum = bottom * bottom if bottom_sum is None else bottom_sum + bottom * bottom
        top_gap = 2.0 * (top_sum - measured[low_rows, :])
        bottom_gap = 2.0 * (bottom_sum - measured[high_rows, :])

        def fold(value):
            return jnp.concatenate(
                [value[:, :HALF] + value[:, HALF:], value[:, :HALF] - value[:, HALF:]], axis=1
            )

        for mode, part, top, bottom in held:
            top_grad = fold(top_gap * top)
            bottom_grad = fold(bottom_gap * bottom)
            at = pl.ds(pl.multiple_of(part * HALF + start, STRIP), STRIP)
            cols = pl.ds(mode * DET, DET)
            for block, both in ((0, top_grad + bottom_grad), (1, top_grad - bottom_grad)):
                z_high[block, at, cols], z_low[block, at, cols] = split(both)
                if last:
                    running = running + both * derived_result[block, at, cols]
        return running

    zeros = jnp.zeros((STRIP, DET), F32) if last else 0
    slope_rows = lax.fori_loop(0, HALF // STRIP, misfits, zeros)

    for block in range(2):
        for mode in range(MODES):
            times_left(block, mode, turned0, z_result)

    def blocks_to_rows(step, _):
        start = pl.multiple_of(step * STRIP, STRIP)
        for mode in range(MODES):
            cols = pl.ds(mode * DET, DET)
            tops, bottoms = [], []
            for part in range(2):
                at = pl.ds(pl.multiple_of(part * HALF + start, STRIP), STRIP)
                even, odd = z_result[0, at, cols], z_result[1, at, cols]
                tops.append(even + odd)
                bottoms.append(even - odd)
            for offset, pair in ((0, tops), (HALF, bottoms)):
                at = pl.ds(pl.multiple_of(mode * DET + offset + start, STRIP), STRIP)
                for block in range(2):
                    lanes = slice(block * HALF, (block + 1) * HALF)
                    both = jnp.concatenate([pair[0][:, lanes], pair[1][:, lanes]], axis=1)
                    high[block, at, :], low[block, at, :] = split(both)
        return 0

    lax.fori_loop(0, HALF // STRIP, blocks_to_rows, 0)

    for block in range(2):
        for mode in range(MODES):
            times_right(block, mode, plain1, result)

    def leave(step, running):
        start = pl.multiple_of(step * STRIP, STRIP)
        rows = pl.ds(start, STRIP)
        real, imag = field[0, rows, :], field[1, rows, :]
        grad_real = jnp.zeros((STRIP, DET), F32)
        grad_imag = jnp.zeros((STRIP, DET), F32)
        for mode in range(MODES):
            at = pl.ds(pl.multiple_of(mode * DET + start, STRIP), STRIP)
            even, odd = result[0, at, :], result[1, at, :]
            if last:
                running = running + even * slope_result[0, at, :] + odd * slope_result[1, at, :]
            plus, minus = even + odd, even - odd
            exit_real = jnp.concatenate([plus[:, :HALF], minus[:, :HALF]], axis=1)
            exit_imag = jnp.concatenate([plus[:, HALF:], minus[:, HALF:]], axis=1)
            probe_real = modes[0, mode, rows, :]
            probe_imag = modes[1, mode, rows, :]
            grad_real = grad_real + probe_real * exit_real + probe_imag * exit_imag
            grad_imag = grad_imag + probe_real * exit_imag - probe_imag * exit_real
            mode_real = real * exit_real + imag * exit_imag
            mode_imag = real * exit_imag - imag * exit_real
            keep_out[mode, rows, :] = jnp.where(core == 0, mode_real, mode_imag)
            send_out[mode, rows, :] = jnp.where(core == 0, mode_imag, mode_real)
        again = pl.ds(pl.multiple_of(start + DET, STRIP), STRIP)
        for part, value in ((0, grad_real), (1, grad_imag)):
            turned = pltpu.roll(value, col0, 1)
            doubled[part, rows, :] = turned
            doubled[part, again, :] = turned
        return running

    slope_cols = lax.fori_loop(0, DET // STRIP, leave, zeros)

    def wrap(step, _):
        start = pl.multiple_of(step * STRIP, STRIP)
        rows = pl.ds(start, STRIP)
        for part in range(2):
            value = rows_from(part, DET - row0 + start)
            if last:
                value = value + grad_before[part, rows, :]
            grad_out[part, rows, :] = value
        return 0

    lax.fori_loop(0, DET // STRIP, wrap, 0)

    if last:
        lane = lax.broadcasted_iota(jnp.int32, (8, HALF), 1)
        shift_out[...] = jnp.where(lane == 0, jnp.sum(slope_rows), 2.0 * jnp.sum(slope_cols)) / DET


def gradient_call(last, rate, scalars, operands):
    plane = jax.ShapeDtypeStruct((2, DET, DET), F32)
    half = jax.ShapeDtypeStruct((MODES, DET, DET), F32)
    vmem = pl.BlockSpec(memory_space=pltpu.VMEM)
    if last:
        outs = (
            plane,
            jax.ShapeDtypeStruct((2, MODES, DET, DET), F32),
            half,
            half,
            jax.ShapeDtypeStruct((8, HALF), F32),
        )
    else:
        outs = (plane, plane, half, half)
    scratch = [
        pltpu.VMEM((2, 2 * DET + 8, DET), F32),
        pltpu.VMEM((2, DET, DET), F32),
        pltpu.VMEM((2, MODES * DET, DET), BF16),
        pltpu.VMEM((2, MODES * DET, DET), BF16),
        pltpu.VMEM((2, MODES * DET, DET), F32),
        pltpu.VMEM((2, DET, MODES * DET), BF16),
        pltpu.VMEM((2, DET, MODES * DET), BF16),
        pltpu.VMEM((2, DET, MODES * DET), F32),
    ]
    if last:
        scratch += [
            pltpu.VMEM((2, MODES * DET, DET), F32),
            pltpu.VMEM((2, DET, MODES * DET), F32),
        ]

    def body(*refs):
        gradient_kernel(last, rate, *refs)

    return pl.pallas_call(
        body,
        out_shape=outs,
        in_specs=[pl.BlockSpec(memory_space=pltpu.SMEM)] + [vmem] * len(operands),
        out_specs=(vmem,) * len(outs),
        scratch_shapes=scratch,
        compiler_params=pltpu.CompilerParams(vmem_limit_bytes=40 * 2**20),
        name="gradient_last" if last else "gradient_first",
    )(scalars, *operands)


def shifted(value, axis, steps):
    count = lax.axis_size(axis)
    initial, last = (max(0, -steps), min(count, count - steps))
    return lax.ppermute(value, axis, [(source, source + steps) for source in range(initial, last)])


def swapped(value, axis, distance):
    count = lax.axis_size(axis)
    return lax.ppermute(value, axis, [(source, source ^ distance) for source in range(count)])


def reduced(keep, send):
    count = lax.axis_size("tile")
    summed = keep + swapped(send, "frame", 1)
    parts = summed.reshape(count, MODES * DET // count, DET)
    parts = lax.all_to_all(parts, "tile", 0, 0)
    part = jnp.sum(parts, axis=0)
    distance = 2
    while distance < lax.axis_size("frame"):
        part = part + swapped(part, "frame", distance)
        distance *= 2
    return part


def spread(part):
    count = lax.axis_size("tile")
    parts = jnp.broadcast_to(part[None], (count,) + part.shape)
    mine = lax.all_to_all(parts, "tile", 0, 0).reshape(MODES, DET, DET)
    return mine, swapped(mine, "frame", 1)


def per_device(object_field, probe_modes, measured, offsets, ramp_steps):
    tile_at, frame_at = lax.axis_index("tile"), lax.axis_index("frame")
    tile_last = lax.axis_size("tile") - 1
    frame_last = lax.axis_size("frame") - 1
    core = frame_at % 2
    rate = probe_step / (lax.axis_size("tile") * lax.axis_size("frame"))
    plain, turned, derived, slope = (jnp.asarray(table) for table in shift_tables())
    steps = ramp_steps[0]
    pick = lambda table, step: lax.dynamic_index_in_dim(table, step, 0, keepdims=False)
    plain0, turned0 = pick(plain, steps[0]), pick(turned, steps[0])
    plain1, turned1 = pick(plain, steps[1]), pick(turned, steps[1])
    derived0 = pick(derived, steps[0])

    here = offsets[0]
    above = shifted(offsets, "tile", 1)[0]
    below = shifted(offsets, "tile", -1)[0]
    left = shifted(offsets, "frame", 1)[0]
    right = shifted(offsets, "frame", -1)[0]
    scalars = jnp.stack(
        [
            here[0],
            here[1],
            core,
            (tile_at == tile_last).astype(jnp.int32),
            (frame_at == frame_last).astype(jnp.int32),
        ]
    )
    row = lax.broadcasted_iota(jnp.int32, (2, DET, DET), 1)
    col = lax.broadcasted_iota(jnp.int32, (2, DET, DET), 2)

    right_tile = shifted(object_field, "frame", -1)
    lower = shifted(jnp.where(col >= above[1], object_field, right_tile), "tile", -1)

    frame = measured[0]
    grad1, patch, keep1, send1 = gradient_call(
        False,
        rate,
        scalars,
        (object_field, right_tile, lower, probe_modes, frame, plain0, turned0, plain1, turned1),
    )

    grad_left = shifted(grad1, "frame", 1)
    grad_right = shifted(grad1, "frame", -1)
    left_cells = col < left[1]
    right_cells = col >= right[1]
    side_left = jnp.where(left_cells, grad_left, 0.0)
    side_right = jnp.where(right_cells, grad_right, 0.0)

    def rows_of(wanted, edge, value):
        return jnp.where((row < edge) == wanted, value, 0.0)

    def gathered(wanted, start):
        kept = rows_of(wanted, here[0], grad1)
        near = jnp.where(col >= here[1], kept, 0.0) + rows_of(wanted, left[0], side_left)
        far = jnp.where(col < here[1], kept, 0.0) + rows_of(wanted, right[0], side_right)
        return jnp.where(col >= start, near, far)

    inside = row < here[0]
    merged = grad1 + jnp.where(
        col >= here[1],
        jnp.where(inside == (row < left[0]), side_left, 0.0),
        jnp.where(inside == (row < right[0]), side_right, 0.0),
    )
    from_above = shifted(gathered(True, below[1]), "tile", 1)
    from_below = shifted(gathered(False, above[1]), "tile", -1)

    mine, other = spread(reduced(keep1, send1))

    grad_total, modes_now, keep2, send2, shift_grad = gradient_call(
        True,
        rate,
        scalars,
        (patch, merged, from_above, from_below, grad1, mine, other)
        + (probe_modes, frame, plain0, turned0, plain1, turned1, derived0, slope),
    )

    moved = shifted(jnp.where(row < here[0], grad_total, 0.0), "tile", 1)
    own_rows = jnp.where(row >= here[0], grad_total, 0.0)
    to_right = jnp.where(col < here[1], own_rows, 0.0) + jnp.where(col < above[1], moved, 0.0)
    stays = jnp.where(col >= here[1], own_rows, 0.0) + jnp.where(col >= above[1], moved, 0.0)
    object_final = object_field - object_step * (stays + shifted(to_right, "frame", 1))

    mine, other = spread(reduced(keep2, send2))
    first = jnp.where(core == 0, mine, other)
    second = jnp.where(core == 0, other, mine)
    probe_final = modes_now - rate * jnp.stack([first, second])
    return (object_final, probe_final, shift_grad[:1, :2])


def solution(mesh):
    placed = (
        P(None, "tile", "frame"),
        P(),
        P(("tile", "frame"), None, None),
        P(("tile", "frame"), None),
        P(("tile", "frame"), None),
    )
    return jax.shard_map(
        per_device,
        mesh=mesh,
        in_specs=placed,
        out_specs=(P(None, "tile", "frame"), P(), P(("tile", "frame"), None)),
        check_vma=False,
    )
```

```python
import math

import jax
import jax.numpy as jnp
import numpy as np
from jax import lax
from jax.experimental import pallas as pl
from jax.experimental.pallas import tpu as pltpu
from jax.sharding import PartitionSpec as P

DET = 256
HALF = 128
MODES = 3
RAMPS = 8
STRIP = 16

object_step = 0.05
probe_step = 0.5
fresnel = 0.25

F32 = jnp.float32
BF16 = jnp.bfloat16


def circulant_blocks(eigenvalues):
    counter = np.arange(DET)
    waves = np.exp(2j * np.pi * (np.outer(counter, counter) % DET) / DET)
    column = waves @ eigenvalues / DET
    full = column[(counter[:, None] - counter[None, :]) % DET]
    first, second = full[:HALF, :HALF], full[:HALF, HALF:]

    def real_form(block):
        return np.block([[block.real, -block.imag], [block.imag, block.real]])

    return np.stack([real_form((first + second) / 2), real_form((first - second) / 2)])


def split_table(table):
    table = table.astype(np.float32)
    high = table.astype(BF16)
    low = (table - high.astype(np.float32)).astype(BF16)
    return np.stack([high, low], axis=-3)


def shift_tables():
    counter = np.arange(DET)
    signed = np.where(counter < DET // 2, counter, counter - DET).astype(np.float64)
    chirp = -np.pi * fresnel * signed * signed / DET
    slope = -2j * np.pi * signed / DET
    plain, derived = [], []
    for step in range(RAMPS):
        factor = np.exp(1j * chirp + slope * (step / RAMPS))
        plain.append(circulant_blocks(factor))
        derived.append(circulant_blocks(slope * factor))
    plain, derived = np.stack(plain), np.stack(derived)
    slope_blocks = circulant_blocks(slope)
    turned = np.swapaxes(plain, -1, -2)
    order = (plain, turned, derived, np.swapaxes(slope_blocks, -1, -2)[None])
    return np.concatenate([split_table(table) for table in order])


def split(value):
    high = value.astype(BF16)
    return high, (value - high.astype(F32)).astype(BF16)


def product(left, right):
    return lax.dot_general(
        left, right, (((1,), (0,)), ((), ())), preferred_element_type=F32
    )


def gradient_kernel(last, rate, *refs):
    refs = list(refs)
    take = lambda count: [refs.pop(0) for _ in range(count)]
    corner, ramp, place = take(3)
    if last:
        patch_in, merged, from_above, from_below, grad_before = take(5)
        total_mine, total_other = take(2)
    else:
        own, first_low, first_side, second_low, second_side = take(5)
    probe_kept, measured_kept, tables = take(3)
    if last:
        grad_out, probe_out, keep_out, send_out, shift_out = take(5)
    else:
        grad_out, patch_out, keep_out, send_out = take(4)
    doubled, field, high, low, result, z_high, z_low, z_result = take(8)
    if last:
        slope_result, derived_result = take(2)
    probe, measured, plain0, turned0, plain1, turned1 = take(6)
    if last:
        derived0, slope1 = take(2)
    (arrived,) = take(1)

    row0, col0, core = corner[0, 0], corner[0, 1], place[0]
    step0, step1 = ramp[0, 0], ramp[0, 1]
    moves = [
        (probe_kept, probe),
        (tables.at[RAMPS + step1], turned1),
        (tables.at[step0], plain0),
        (measured_kept.at[0], measured),
        (tables.at[RAMPS + step0], turned0),
        (tables.at[step1], plain1),
    ]
    if last:
        moves += [(tables.at[2 * RAMPS + step0], derived0), (tables.at[3 * RAMPS], slope1)]
    copies = [
        pltpu.make_async_copy(source, target, arrived.at[index])
        for index, (source, target) in enumerate(moves)
    ]
    for copy in copies:
        copy.start()

    def build(step, _):
        start = pl.multiple_of(step * STRIP, STRIP)
        rows = pl.ds(start, STRIP)
        again = pl.ds(start + DET, STRIP)
        row_at = lax.broadcasted_iota(jnp.int32, (STRIP, DET), 0) + start
        col_at = lax.broadcasted_iota(jnp.int32, (STRIP, DET), 1)
        if last:
            outside = ((row_at < row0) & (place[1] == 1)) | ((col_at < col0) & (place[2] == 1))
        for part in range(2):
            if last:
                moved = jnp.where(row_at >= row0, from_above[part, rows, :], from_below[part, rows, :])
                cells = patch_in[part, rows, :] - object_step * (merged[part, rows, :] + moved)
                cells = jnp.where(outside, 0.0, cells)
            else:
                mine = own[part, rows, :]
                if part == 0:
                    column = jnp.where(row_at >= row0, mine, first_low[rows, :])
                    cells = jnp.where(col_at >= col0, column, first_side[rows, :])
                else:
                    line = jnp.where(col_at >= col0, mine, second_side[rows, :])
                    cells = jnp.where(row_at >= row0, line, second_low[rows, :])
                patch_out[part, rows, :] = cells
            doubled[part, rows, :] = cells
            doubled[part, again, :] = cells
        if last:
            for mode in range(MODES):
                mine = total_mine[mode, rows, :]
                other = total_other[mode, rows, :]
                probe_out[0, mode, rows, :] = probe[0, mode, rows, :] - rate * jnp.where(core == 0, mine, other)
                probe_out[1, mode, rows, :] = probe[1, mode, rows, :] - rate * jnp.where(core == 0, other, mine)
        return 0

    if last:
        copies[0].wait()
    lax.fori_loop(0, DET // STRIP, build, 0)
    if not last:
        copies[0].wait()
    modes = probe_out if last else probe
    back = lax.rem(DET - col0, DET)

    def rows_from(part, first):
        down = lax.rem(first, 8)
        at = pl.ds(pl.multiple_of(first - down, 8), STRIP + 8)
        return pltpu.roll(doubled[part, at, :], lax.rem(STRIP + 8 - down, STRIP + 8), 0)[:STRIP]

    def enter(step, _):
        start = pl.multiple_of(step * STRIP, STRIP)
        rows = pl.ds(start, STRIP)
        real = pltpu.roll(rows_from(0, row0 + start), back, 1)
        imag = pltpu.roll(rows_from(1, row0 + start), back, 1)
        field[0, rows, :] = real
        field[1, rows, :] = imag
        for mode in range(MODES):
            probe_real = modes[0, mode, rows, :]
            probe_imag = modes[1, mode, rows, :]
            exit_real = probe_real * real - probe_imag * imag
            exit_imag = probe_real * imag + probe_imag * real
            at = pl.ds(pl.multiple_of(mode * DET + start, STRIP), STRIP)
            for block, sign in ((0, 1.0), (1, -1.0)):
                both = jnp.concatenate(
                    [
                        exit_real[:, :HALF] + sign * exit_real[:, HALF:],
                        exit_imag[:, :HALF] + sign * exit_imag[:, HALF:],
                    ],
                    axis=1,
                )
                high[block, at, :], low[block, at, :] = split(both)
        return 0

    lax.fori_loop(0, DET // STRIP, enter, 0)
    for copy in copies[1:]:
        copy.wait()

    def times_right(block, mode, table, where):
        at = pl.ds(mode * DET, DET)
        left_high, left_low = high[block, at, :], low[block, at, :]
        where[block, at, :] = (
            product(left_high, table[block, 0])
            + product(left_low, table[block, 0])
            + product(left_high, table[block, 1])
        )

    def times_left(block, mode, table, where):
        at = pl.ds(mode * DET, DET)
        right_high, right_low = z_high[block, :, at], z_low[block, :, at]
        where[block, :, at] = (
            product(table[block, 0], right_high)
            + product(table[block, 0], right_low)
            + product(table[block, 1], right_high)
        )

    for block in range(2):
        for mode in range(MODES):
            times_right(block, mode, turned1, result)
            if last:
                times_right(block, mode, slope1, slope_result)

    def rows_to_blocks(step, _):
        start = pl.multiple_of(step * STRIP, STRIP)
        for mode in range(MODES):
            top = pl.ds(pl.multiple_of(mode * DET + start, STRIP), STRIP)
            bottom = pl.ds(pl.multiple_of(mode * DET + HALF + start, STRIP), STRIP)
            sums = [(result[col, top, :] + result[col, bottom, :]) for col in range(2)]
            gaps = [(result[col, top, :] - result[col, bottom, :]) for col in range(2)]
            for block, pair in ((0, sums), (1, gaps)):
                for part in range(2):
                    lanes = slice(part * HALF, (part + 1) * HALF)
                    both = jnp.concatenate([pair[0][:, lanes], pair[1][:, lanes]], axis=1)
                    at = pl.ds(pl.multiple_of(part * HALF + start, STRIP), STRIP)
                    cols = pl.ds(mode * DET, DET)
                    z_high[block, at, cols], z_low[block, at, cols] = split(both)
        return 0

    lax.fori_loop(0, HALF // STRIP, rows_to_blocks, 0)

    for block in range(2):
        for mode in range(MODES):
            times_left(block, mode, plain0, z_result)
            if last:
                times_left(block, mode, derived0, derived_result)

    def misfits(step, running):
        start = pl.multiple_of(step * STRIP, STRIP)
        low_rows = pl.ds(start, STRIP)
        high_rows = pl.ds(pl.multiple_of(start + HALF, STRIP), STRIP)

        def waves(mode, part):
            at = pl.ds(pl.multiple_of(part * HALF + start, STRIP), STRIP)
            cols = pl.ds(mode * DET, DET)
            even, odd = z_result[0, at, cols], z_result[1, at, cols]

            def spread(value):
                return jnp.concatenate(
                    [value[:, :HALF] + value[:, HALF:], value[:, :HALF] - value[:, HALF:]], axis=1
                )

            return spread(even + odd), spread(even - odd)

        top_sum = bottom_sum = None
        held = []
        for mode in range(MODES):
            for part in range(2):
                top, bottom = waves(mode, part)
                held.append((mode, part, top, bottom))
                top_sum = top * top if top_sum is None else top_sum + top * top
                bottom_sum = bottom * bottom if bottom_sum is None else bottom_sum + bottom * bottom
        top_gap = 2.0 * (top_sum - measured[low_rows, :])
        bottom_gap = 2.0 * (bottom_sum - measured[high_rows, :])

        def fold(value):
            return jnp.concatenate(
                [value[:, :HALF] + value[:, HALF:], value[:, :HALF] - value[:, HALF:]], axis=1
            )

        for mode, part, top, bottom in held:
            top_grad = fold(top_gap * top)
            bottom_grad = fold(bottom_gap * bottom)
            at = pl.ds(pl.multiple_of(part * HALF + start, STRIP), STRIP)
            cols = pl.ds(mode * DET, DET)
            for block, both in ((0, top_grad + bottom_grad), (1, top_grad - bottom_grad)):
                z_high[block, at, cols], z_low[block, at, cols] = split(both)
                if last:
                    running = running + both * derived_result[block, at, cols]
        return running

    zeros = jnp.zeros((STRIP, DET), F32) if last else 0
    slope_rows = lax.fori_loop(0, HALF // STRIP, misfits, zeros)

    for block in range(2):
        for mode in range(MODES):
            times_left(block, mode, turned0, z_result)

    def blocks_to_rows(step, _):
        start = pl.multiple_of(step * STRIP, STRIP)
        for mode in range(MODES):
            cols = pl.ds(mode * DET, DET)
            tops, bottoms = [], []
            for part in range(2):
                at = pl.ds(pl.multiple_of(part * HALF + start, STRIP), STRIP)
                even, odd = z_result[0, at, cols], z_result[1, at, cols]
                tops.append(even + odd)
                bottoms.append(even - odd)
            for offset, pair in ((0, tops), (HALF, bottoms)):
                at = pl.ds(pl.multiple_of(mode * DET + offset + start, STRIP), STRIP)
                for block in range(2):
                    lanes = slice(block * HALF, (block + 1) * HALF)
                    both = jnp.concatenate([pair[0][:, lanes], pair[1][:, lanes]], axis=1)
                    high[block, at, :], low[block, at, :] = split(both)
        return 0

    lax.fori_loop(0, HALF // STRIP, blocks_to_rows, 0)

    for block in range(2):
        for mode in range(MODES):
            times_right(block, mode, plain1, result)

    def leave(step, running):
        start = pl.multiple_of(step * STRIP, STRIP)
        rows = pl.ds(start, STRIP)
        real, imag = field[0, rows, :], field[1, rows, :]
        grad_real = jnp.zeros((STRIP, DET), F32)
        grad_imag = jnp.zeros((STRIP, DET), F32)
        for mode in range(MODES):
            at = pl.ds(pl.multiple_of(mode * DET + start, STRIP), STRIP)
            even, odd = result[0, at, :], result[1, at, :]
            if last:
                running = running + even * slope_result[0, at, :] + odd * slope_result[1, at, :]
            plus, minus = even + odd, even - odd
            exit_real = jnp.concatenate([plus[:, :HALF], minus[:, :HALF]], axis=1)
            exit_imag = jnp.concatenate([plus[:, HALF:], minus[:, HALF:]], axis=1)
            probe_real = modes[0, mode, rows, :]
            probe_imag = modes[1, mode, rows, :]
            grad_real = grad_real + probe_real * exit_real + probe_imag * exit_imag
            grad_imag = grad_imag + probe_real * exit_imag - probe_imag * exit_real
            mode_real = real * exit_real + imag * exit_imag
            mode_imag = real * exit_imag - imag * exit_real
            keep_out[mode, rows, :] = jnp.where(core == 0, mode_real, mode_imag)
            send_out[mode, rows, :] = jnp.where(core == 0, mode_imag, mode_real)
        again = pl.ds(pl.multiple_of(start + DET, STRIP), STRIP)
        for part, value in ((0, grad_real), (1, grad_imag)):
            turned = pltpu.roll(value, col0, 1)
            doubled[part, rows, :] = turned
            doubled[part, again, :] = turned
        return running

    slope_cols = lax.fori_loop(0, DET // STRIP, leave, zeros)

    def wrap(step, _):
        start = pl.multiple_of(step * STRIP, STRIP)
        rows = pl.ds(start, STRIP)
        for part in range(2):
            value = rows_from(part, DET - row0 + start)
            if last:
                value = value + grad_before[part, rows, :]
            grad_out[part, rows, :] = value
        return 0

    lax.fori_loop(0, DET // STRIP, wrap, 0)

    if last:
        lane = lax.broadcasted_iota(jnp.int32, (8, HALF), 1)
        shift_out[...] = jnp.where(lane == 0, jnp.sum(slope_rows), 2.0 * jnp.sum(slope_cols)) / DET


def gradient_call(last, rate, scalars, operands, kept):
    plane = jax.ShapeDtypeStruct((2, DET, DET), F32)
    half = jax.ShapeDtypeStruct((MODES, DET, DET), F32)
    vmem = pl.BlockSpec(memory_space=pltpu.VMEM)
    smem = pl.BlockSpec(memory_space=pltpu.SMEM)
    if last:
        outs = (
            plane,
            jax.ShapeDtypeStruct((2, MODES, DET, DET), F32),
            half,
            half,
            jax.ShapeDtypeStruct((8, HALF), F32),
        )
    else:
        outs = (plane, plane, half, half)
    scratch = [
        pltpu.VMEM((2, 2 * DET + 8, DET), F32),
        pltpu.VMEM((2, DET, DET), F32),
        pltpu.VMEM((2, MODES * DET, DET), BF16),
        pltpu.VMEM((2, MODES * DET, DET), BF16),
        pltpu.VMEM((2, MODES * DET, DET), F32),
        pltpu.VMEM((2, DET, MODES * DET), BF16),
        pltpu.VMEM((2, DET, MODES * DET), BF16),
        pltpu.VMEM((2, DET, MODES * DET), F32),
    ]
    if last:
        scratch += [
            pltpu.VMEM((2, MODES * DET, DET), F32),
            pltpu.VMEM((2, DET, MODES * DET), F32),
        ]
    scratch += [pltpu.VMEM((2, MODES, DET, DET), F32), pltpu.VMEM((DET, DET), F32)]
    tables = 6 if last else 4
    scratch += [pltpu.VMEM((2, 2, DET, DET), BF16)] * tables
    scratch += [pltpu.SemaphoreType.DMA((tables + 2,))]

    def body(*refs):
        gradient_kernel(last, rate, *refs)

    return pl.pallas_call(
        body,
        out_shape=outs,
        in_specs=[smem] * len(scalars)
        + [vmem] * len(operands)
        + [pl.BlockSpec(memory_space=pltpu.HBM)] * len(kept),
        out_specs=(vmem,) * len(outs),
        scratch_shapes=scratch,
        compiler_params=pltpu.CompilerParams(vmem_limit_bytes=(44 if last else 46) * 2**20),
        name="gradient_last" if last else "gradient_first",
    )(*scalars, *operands, *kept)


def plane_call(name, body, scalars, operands, outputs):
    def kernel(*refs):
        at_scalars, refs = refs[: len(scalars)], refs[len(scalars) :]

        def strip(step, _):
            start = pl.multiple_of(step * STRIP, STRIP)
            row = lax.broadcasted_iota(jnp.int32, (STRIP, DET), 0) + start
            col = lax.broadcasted_iota(jnp.int32, (STRIP, DET), 1)
            for part in range(2):
                at = (part, pl.ds(start, STRIP), slice(None))
                values = [ref[at] for ref in refs[: len(operands)]]
                for ref, value in zip(refs[len(operands) :], body(at_scalars, row, col, *values)):
                    ref[at] = value
            return 0

        lax.fori_loop(0, DET // STRIP, strip, 0)

    vmem = pl.BlockSpec(memory_space=pltpu.VMEM)
    return pl.pallas_call(
        kernel,
        out_shape=[jax.ShapeDtypeStruct((2, DET, DET), F32)] * outputs,
        in_specs=[pl.BlockSpec(memory_space=pltpu.SMEM)] * len(scalars) + [vmem] * len(operands),
        out_specs=[vmem] * outputs,
        compiler_params=pltpu.CompilerParams(vmem_limit_bytes=8 * 2**20),
        name=name,
    )(*scalars, *operands)


def side_kernel(left_at, above_at, own, lower, right, to_left, to_above):
    def strip(step, _):
        start = pl.multiple_of(step * STRIP, STRIP)
        rows = pl.ds(start, STRIP)
        row = lax.broadcasted_iota(jnp.int32, (STRIP, DET), 0) + start
        col = lax.broadcasted_iota(jnp.int32, (STRIP, DET), 1)
        to_left[rows, :] = jnp.where(row >= left_at[0, 0], own[0, rows, :], lower[rows, :])
        to_above[rows, :] = jnp.where(col >= above_at[0, 1], own[1, rows, :], right[rows, :])
        return 0

    lax.fori_loop(0, DET // STRIP, strip, 0)


def side_call(left_at, above_at, own, lower, right):
    vmem = pl.BlockSpec(memory_space=pltpu.VMEM)
    return pl.pallas_call(
        side_kernel,
        out_shape=[jax.ShapeDtypeStruct((DET, DET), F32)] * 2,
        in_specs=[pl.BlockSpec(memory_space=pltpu.SMEM)] * 2 + [vmem] * 3,
        out_specs=[vmem] * 2,
        compiler_params=pltpu.CompilerParams(vmem_limit_bytes=8 * 2**20),
        name="sides",
    )(left_at, above_at, own, lower, right)


def merge_cells(corners, row, col, own, left, right):
    here_at, left_at, right_at, above_at, below_at = corners
    inside = row < here_at[0, 0]
    inside_left = row < left_at[0, 0]
    inside_right = row < right_at[0, 0]
    near = col >= here_at[0, 1]
    left = jnp.where(col < left_at[0, 1], left, 0.0)
    right = jnp.where(col >= right_at[0, 1], right, 0.0)
    own_near = jnp.where(near, own, 0.0)
    own_far = jnp.where(near, 0.0, own)

    def gathered(wanted, start):
        near_sum = jnp.where(inside == wanted, own_near, 0.0) + jnp.where(inside_left == wanted, left, 0.0)
        far_sum = jnp.where(inside == wanted, own_far, 0.0) + jnp.where(inside_right == wanted, right, 0.0)
        return jnp.where(col >= start, near_sum, far_sum)

    merged = own + jnp.where(
        near,
        jnp.where(inside == inside_left, left, 0.0),
        jnp.where(inside == inside_right, right, 0.0),
    )
    return merged, gathered(True, below_at[0, 1]), gathered(False, above_at[0, 1])


def settle_cells(corners, row, col, own, left):
    here_at, left_at = corners
    own = jnp.where(col >= here_at[0, 1], own, 0.0)
    left = jnp.where(col < left_at[0, 1], left, 0.0)
    own_here, left_here = row >= here_at[0, 0], row >= left_at[0, 0]
    down = jnp.where(own_here, 0.0, own) + jnp.where(left_here, 0.0, left)
    stays = jnp.where(own_here, own, 0.0) + jnp.where(left_here, left, 0.0)
    return down, stays


def shifted(value, axis, steps):
    count = lax.axis_size(axis)
    initial, last = (max(0, -steps), min(count, count - steps))
    return lax.ppermute(value, axis, [(source, source + steps) for source in range(initial, last)])


def swapped(value, axis, distance):
    count = lax.axis_size(axis)
    return lax.ppermute(value, axis, [(source, source ^ distance) for source in range(count)])


def tile_sum(keep, send):
    count = lax.axis_size("tile")
    summed = keep + swapped(send, "frame", 1)
    parts = summed.reshape(count, MODES * DET // count, DET)
    return jnp.sum(lax.all_to_all(parts, "tile", 0, 0), axis=0)


def chip_sum(part):
    distance = 2
    while distance < lax.axis_size("frame"):
        part = part + swapped(part, "frame", distance)
        distance *= 2
    return part


def spread(part):
    count = lax.axis_size("tile")
    parts = jnp.broadcast_to(part[None], (count,) + part.shape)
    mine = lax.all_to_all(parts, "tile", 0, 0).reshape(MODES, DET, DET)
    return mine, swapped(mine, "frame", 1)


def per_device(object_field, probe_modes, measured, offsets, ramp_steps):
    tile_at, frame_at = lax.axis_index("tile"), lax.axis_index("frame")
    core = frame_at & 1
    place = jnp.stack(
        [
            core,
            (tile_at == lax.axis_size("tile") - 1).astype(jnp.int32),
            (frame_at == lax.axis_size("frame") - 1).astype(jnp.int32),
        ]
    )
    rate = probe_step / (lax.axis_size("tile") * lax.axis_size("frame"))
    together = lax.optimization_barrier

    lower = shifted(object_field[0], "tile", -1)
    right = shifted(object_field[1], "frame", -1)
    at_left = shifted(offsets, "frame", 1)
    at_above = shifted(offsets, "tile", 1)
    lower, right, at_left, at_above = together((lower, right, at_left, at_above))
    to_left, to_above = side_call(at_left, at_above, object_field, lower, right)
    side = shifted(to_left, "frame", -1)
    below = shifted(to_above, "tile", -1)

    scalars = (offsets, ramp_steps, place)
    kept = (probe_modes, measured, jnp.asarray(shift_tables()))
    grad1, patch, keep1, send1 = gradient_call(
        False, rate, scalars, (object_field, lower, side, below, right), kept
    )

    grad_left = shifted(grad1, "frame", 1)
    grad_right = shifted(grad1, "frame", -1)
    keep1, send1, corner = together((keep1, send1, offsets))
    at_right = shifted(corner, "frame", -1)
    at_below = shifted(corner, "tile", -1)
    part = tile_sum(keep1, send1)
    part, grad_left, grad_right, at_right, at_below = together((part, grad_left, grad_right, at_right, at_below))
    merged, down, up = plane_call(
        "merge", merge_cells, (offsets, at_left, at_right, at_above, at_below), (grad1, grad_left, grad_right), 3
    )
    part, down, up = together((part, down, up))
    from_above = shifted(down, "tile", 1)
    from_below = shifted(up, "tile", -1)
    part, from_above, from_below = together((chip_sum(part), from_above, from_below))
    mine, other = spread(part)

    grad_total, modes_now, keep2, send2, shift_grad = gradient_call(
        True,
        rate,
        scalars,
        (patch, merged, from_above, from_below, grad1, mine, other),
        kept,
    )

    count = lax.axis_size("tile")
    planes = modes_now.reshape(2, count, MODES * DET // count, DET)
    own_part = lax.dynamic_slice(planes, (core, tile_at, 0, 0), (1, 1) + planes.shape[2:])[0, 0]

    moved = shifted(grad_total, "frame", 1)
    part = tile_sum(keep2, send2)
    part, moved = together((part, moved))
    down, stays = plane_call(
        "settle", settle_cells, (offsets, at_left), (grad_total, moved), 2
    )
    part, down = together((part, down))
    arrived = shifted(down, "tile", 1)
    part = own_part - rate * chip_sum(part)
    part, arrived = together((part, arrived))
    object_final = object_field - object_step * (stays + arrived)

    mine, other = spread(part)
    plane = lax.broadcasted_iota(jnp.int32, (2, MODES, DET, DET), 0)
    probe_final = jnp.where(plane == core, mine[None], other[None])
    return (object_final, probe_final, shift_grad[:1, :2])


def solution(mesh):
    placed = (
        P(None, "tile", "frame"),
        P(),
        P(("tile", "frame"), None, None),
        P(("tile", "frame"), None),
        P(("tile", "frame"), None),
    )
    return jax.shard_map(
        per_device,
        mesh=mesh,
        in_specs=placed,
        out_specs=(P(None, "tile", "frame"), P(), P(("tile", "frame"), None)),
        check_vma=False,
    )
```

```python
import math

import jax
import jax.numpy as jnp
import numpy as np
from jax import lax
from jax.experimental import pallas as pl
from jax.experimental.pallas import tpu as pltpu
from jax.sharding import PartitionSpec as P

DET = 256
HALF = 128
MODES = 3
RAMPS = 8
STRIP = 16
FIRST = 384

object_step = 0.05
probe_step = 0.5
fresnel = 0.25

WEIGHT = 2 * 10**10

F32 = jnp.float32
BF16 = jnp.bfloat16


def circulant_blocks(eigenvalues):
    counter = np.arange(DET)
    waves = np.exp(2j * np.pi * (np.outer(counter, counter) % DET) / DET)
    column = waves @ eigenvalues / DET
    full = column[(counter[:, None] - counter[None, :]) % DET]
    first, second = full[:HALF, :HALF], full[:HALF, HALF:]

    def real_form(block):
        return np.block([[block.real, -block.imag], [block.imag, block.real]])

    return np.stack([real_form((first + second) / 2), real_form((first - second) / 2)])


def split_table(table):
    table = table.astype(np.float32)
    high = table.astype(BF16)
    low = (table - high.astype(np.float32)).astype(BF16)
    return np.stack([high, low], axis=-3)


def shift_tables():
    counter = np.arange(DET)
    signed = np.where(counter < DET // 2, counter, counter - DET).astype(np.float64)
    chirp = -np.pi * fresnel * signed * signed / DET
    slope = -2j * np.pi * signed / DET
    plain, derived = [], []
    for step in range(RAMPS):
        factor = np.exp(1j * chirp + slope * (step / RAMPS))
        plain.append(circulant_blocks(factor))
        derived.append(circulant_blocks(slope * factor))
    plain, derived = np.stack(plain), np.stack(derived)
    slope_blocks = circulant_blocks(slope)
    turned = np.swapaxes(plain, -1, -2)
    order = (plain, turned, derived, np.swapaxes(slope_blocks, -1, -2)[None])
    return np.concatenate([split_table(table) for table in order])


def split(value):
    high = value.astype(BF16)
    return high, (value - high.astype(F32)).astype(BF16)


def product(left, right):
    return lax.dot_general(
        left, right, (((1,), (0,)), ((), ())), preferred_element_type=F32
    )


def gradient_kernel(last, rate, *refs):
    refs = list(refs)
    take = lambda count: [refs.pop(0) for _ in range(count)]
    corner, ramp, place = take(3)
    if last:
        patch_in, merged, from_above, from_below, grad_before = take(5)
        total_mine, total_other = take(2)
    else:
        own_first, own_second, lower, right, side, below = take(6)
    probe, measured, tables = take(3)
    if last:
        grad_out, probe_out, keep_out, send_out, shift_out = take(5)
    else:
        grad_out, patch_out, keep_out, send_out = take(4)
    doubled, field, high, low, result, z_high, z_low, z_result = take(8)
    if last:
        slope_result, derived_result = take(2)
    plain0, turned0, plain1, turned1 = take(4)
    if last:
        derived0, slope1 = take(2)
    (arrived,) = take(1)

    row0, col0, core = corner[0, 0], corner[0, 1], place[0]
    step0, step1 = ramp[0, 0], ramp[0, 1]
    moves = [
        (tables.at[RAMPS + step1], turned1),
        (tables.at[step0], plain0),
        (tables.at[RAMPS + step0], turned0),
        (tables.at[step1], plain1),
    ]
    if last:
        moves += [(tables.at[2 * RAMPS + step0], derived0), (tables.at[3 * RAMPS], slope1)]
    copies = [
        pltpu.make_async_copy(source, target, arrived.at[index])
        for index, (source, target) in enumerate(moves)
    ]
    for copy in copies:
        copy.start()

    def build(step):
        start = step * STRIP
        rows = pl.ds(start, STRIP)
        again = pl.ds(start + DET, STRIP)
        row_at = lax.broadcasted_iota(jnp.int32, (STRIP, DET), 0) + start
        col_at = lax.broadcasted_iota(jnp.int32, (STRIP, DET), 1)
        if last:
            outside = ((row_at < row0) & (place[1] == 1)) | ((col_at < col0) & (place[2] == 1))
        for part in range(2):
            if last:
                moved = jnp.where(row_at >= row0, from_above[part, rows, :], from_below[part, rows, :])
                cells = patch_in[part, rows, :] - object_step * (merged[part, rows, :] + moved)
                cells = jnp.where(outside, 0.0, cells)
            else:
                flat = part * DET + step * STRIP
                if flat < FIRST:
                    at = pl.ds(flat, STRIP)
                    column = jnp.where(row_at >= row0, own_first[at, :], lower[at, :])
                    cells = jnp.where(col_at >= col0, column, side[at, :])
                else:
                    at = pl.ds(flat - FIRST, STRIP)
                    line = jnp.where(col_at >= col0, own_second[at, :], right[at, :])
                    cells = jnp.where(row_at >= row0, line, below[at, :])
                patch_out[part, rows, :] = cells
            doubled[part, rows, :] = cells
            doubled[part, again, :] = cells
        if last:
            for mode in range(MODES):
                mine = total_mine[mode, rows, :]
                other = total_other[mode, rows, :]
                probe_out[0, mode, rows, :] = probe[0, mode, rows, :] - rate * jnp.where(core == 0, mine, other)
                probe_out[1, mode, rows, :] = probe[1, mode, rows, :] - rate * jnp.where(core == 0, other, mine)

    for step in range(DET // STRIP):
        build(step)
    modes = probe_out if last else probe
    back = lax.rem(DET - col0, DET)

    def rows_from(part, first):
        down = lax.rem(first, 8)
        at = pl.ds(pl.multiple_of(first - down, 8), STRIP + 8)
        return pltpu.roll(doubled[part, at, :], lax.rem(STRIP + 8 - down, STRIP + 8), 0)[:STRIP]

    def enter(step, _):
        start = pl.multiple_of(step * STRIP, STRIP)
        rows = pl.ds(start, STRIP)
        real = pltpu.roll(rows_from(0, row0 + start), back, 1)
        imag = pltpu.roll(rows_from(1, row0 + start), back, 1)
        field[0, rows, :] = real
        field[1, rows, :] = imag
        for mode in range(MODES):
            probe_real = modes[0, mode, rows, :]
            probe_imag = modes[1, mode, rows, :]
            exit_real = probe_real * real - probe_imag * imag
            exit_imag = probe_real * imag + probe_imag * real
            at = pl.ds(pl.multiple_of(mode * DET + start, STRIP), STRIP)
            for block, sign in ((0, 1.0), (1, -1.0)):
                both = jnp.concatenate(
                    [
                        exit_real[:, :HALF] + sign * exit_real[:, HALF:],
                        exit_imag[:, :HALF] + sign * exit_imag[:, HALF:],
                    ],
                    axis=1,
                )
                high[block, at, :], low[block, at, :] = split(both)
        return 0

    lax.fori_loop(0, DET // STRIP, enter, 0, unroll=16)
    copies[0].wait()
    if last:
        copies[5].wait()

    def times_right(block, mode, table, where):
        at = pl.ds(mode * DET, DET)
        left_high, left_low = high[block, at, :], low[block, at, :]
        where[block, at, :] = (
            product(left_high, table[block, 0])
            + product(left_low, table[block, 0])
            + product(left_high, table[block, 1])
        )

    def times_left(block, mode, table, where):
        at = pl.ds(mode * DET, DET)
        right_high, right_low = z_high[block, :, at], z_low[block, :, at]
        where[block, :, at] = (
            product(table[block, 0], right_high)
            + product(table[block, 0], right_low)
            + product(table[block, 1], right_high)
        )

    for block in range(2):
        for mode in range(MODES):
            times_right(block, mode, turned1, result)
            if last:
                times_right(block, mode, slope1, slope_result)

    def rows_to_blocks(step, _):
        start = pl.multiple_of(step * STRIP, STRIP)
        for mode in range(MODES):
            top = pl.ds(pl.multiple_of(mode * DET + start, STRIP), STRIP)
            bottom = pl.ds(pl.multiple_of(mode * DET + HALF + start, STRIP), STRIP)
            sums = [(result[col, top, :] + result[col, bottom, :]) for col in range(2)]
            gaps = [(result[col, top, :] - result[col, bottom, :]) for col in range(2)]
            for block, pair in ((0, sums), (1, gaps)):
                for part in range(2):
                    lanes = slice(part * HALF, (part + 1) * HALF)
                    both = jnp.concatenate([pair[0][:, lanes], pair[1][:, lanes]], axis=1)
                    at = pl.ds(pl.multiple_of(part * HALF + start, STRIP), STRIP)
                    cols = pl.ds(mode * DET, DET)
                    z_high[block, at, cols], z_low[block, at, cols] = split(both)
        return 0

    lax.fori_loop(0, HALF // STRIP, rows_to_blocks, 0, unroll=8)
    copies[1].wait()
    if last:
        copies[4].wait()

    for block in range(2):
        for mode in range(MODES):
            times_left(block, mode, plain0, z_result)
            if last:
                times_left(block, mode, derived0, derived_result)

    def misfits(step, running):
        start = pl.multiple_of(step * STRIP, STRIP)
        low_rows = pl.ds(start, STRIP)
        high_rows = pl.ds(pl.multiple_of(start + HALF, STRIP), STRIP)

        def waves(mode, part):
            at = pl.ds(pl.multiple_of(part * HALF + start, STRIP), STRIP)
            cols = pl.ds(mode * DET, DET)
            even, odd = z_result[0, at, cols], z_result[1, at, cols]

            def spread(value):
                return jnp.concatenate(
                    [value[:, :HALF] + value[:, HALF:], value[:, :HALF] - value[:, HALF:]], axis=1
                )

            return spread(even + odd), spread(even - odd)

        top_sum = bottom_sum = None
        held = []
        for mode in range(MODES):
            for part in range(2):
                top, bottom = waves(mode, part)
                held.append((mode, part, top, bottom))
                top_sum = top * top if top_sum is None else top_sum + top * top
                bottom_sum = bottom * bottom if bottom_sum is None else bottom_sum + bottom * bottom
        top_gap = 2.0 * (top_sum - measured[0, low_rows, :])
        bottom_gap = 2.0 * (bottom_sum - measured[0, high_rows, :])

        def fold(value):
            return jnp.concatenate(
                [value[:, :HALF] + value[:, HALF:], value[:, :HALF] - value[:, HALF:]], axis=1
            )

        for mode, part, top, bottom in held:
            top_grad = fold(top_gap * top)
            bottom_grad = fold(bottom_gap * bottom)
            at = pl.ds(pl.multiple_of(part * HALF + start, STRIP), STRIP)
            cols = pl.ds(mode * DET, DET)
            for block, both in ((0, top_grad + bottom_grad), (1, top_grad - bottom_grad)):
                z_high[block, at, cols], z_low[block, at, cols] = split(both)
                if last:
                    running = running + both * derived_result[block, at, cols]
        return running

    zeros = jnp.zeros((STRIP, DET), F32) if last else 0
    slope_rows = lax.fori_loop(0, HALF // STRIP, misfits, zeros, unroll=8)
    copies[2].wait()

    for block in range(2):
        for mode in range(MODES):
            times_left(block, mode, turned0, z_result)

    def blocks_to_rows(step, _):
        start = pl.multiple_of(step * STRIP, STRIP)
        for mode in range(MODES):
            cols = pl.ds(mode * DET, DET)
            tops, bottoms = [], []
            for part in range(2):
                at = pl.ds(pl.multiple_of(part * HALF + start, STRIP), STRIP)
                even, odd = z_result[0, at, cols], z_result[1, at, cols]
                tops.append(even + odd)
                bottoms.append(even - odd)
            for offset, pair in ((0, tops), (HALF, bottoms)):
                at = pl.ds(pl.multiple_of(mode * DET + offset + start, STRIP), STRIP)
                for block in range(2):
                    lanes = slice(block * HALF, (block + 1) * HALF)
                    both = jnp.concatenate([pair[0][:, lanes], pair[1][:, lanes]], axis=1)
                    high[block, at, :], low[block, at, :] = split(both)
        return 0

    lax.fori_loop(0, HALF // STRIP, blocks_to_rows, 0, unroll=8)
    copies[3].wait()

    for block in range(2):
        for mode in range(MODES):
            times_right(block, mode, plain1, result)

    def leave(step, running):
        start = pl.multiple_of(step * STRIP, STRIP)
        rows = pl.ds(start, STRIP)
        real, imag = field[0, rows, :], field[1, rows, :]
        grad_real = jnp.zeros((STRIP, DET), F32)
        grad_imag = jnp.zeros((STRIP, DET), F32)
        for mode in range(MODES):
            at = pl.ds(pl.multiple_of(mode * DET + start, STRIP), STRIP)
            even, odd = result[0, at, :], result[1, at, :]
            if last:
                running = running + even * slope_result[0, at, :] + odd * slope_result[1, at, :]
            plus, minus = even + odd, even - odd
            exit_real = jnp.concatenate([plus[:, :HALF], minus[:, :HALF]], axis=1)
            exit_imag = jnp.concatenate([plus[:, HALF:], minus[:, HALF:]], axis=1)
            probe_real = modes[0, mode, rows, :]
            probe_imag = modes[1, mode, rows, :]
            grad_real = grad_real + probe_real * exit_real + probe_imag * exit_imag
            grad_imag = grad_imag + probe_real * exit_imag - probe_imag * exit_real
            mode_real = real * exit_real + imag * exit_imag
            mode_imag = real * exit_imag - imag * exit_real
            keep_out[mode, rows, :] = jnp.where(core == 0, mode_real, mode_imag)
            send_out[mode, rows, :] = jnp.where(core == 0, mode_imag, mode_real)
        again = pl.ds(pl.multiple_of(start + DET, STRIP), STRIP)
        for part, value in ((0, grad_real), (1, grad_imag)):
            turned = pltpu.roll(value, col0, 1)
            doubled[part, rows, :] = turned
            doubled[part, again, :] = turned
        return running

    slope_cols = lax.fori_loop(0, DET // STRIP, leave, zeros, unroll=16)

    def wrap(step, _):
        start = pl.multiple_of(step * STRIP, STRIP)
        rows = pl.ds(start, STRIP)
        for part in range(2):
            value = rows_from(part, DET - row0 + start)
            if last:
                value = value + grad_before[part, rows, :]
            grad_out[part, rows, :] = value
        return 0

    lax.fori_loop(0, DET // STRIP, wrap, 0, unroll=16)

    if last:
        lane = lax.broadcasted_iota(jnp.int32, (8, HALF), 1)
        shift_out[...] = jnp.where(lane == 0, jnp.sum(slope_rows), 2.0 * jnp.sum(slope_cols)) / DET


def gradient_call(last, rate, scalars, operands, kept):
    plane = jax.ShapeDtypeStruct((2, DET, DET), F32)
    half = jax.ShapeDtypeStruct((MODES, DET, DET), F32)
    vmem = pl.BlockSpec(memory_space=pltpu.VMEM)
    smem = pl.BlockSpec(memory_space=pltpu.SMEM)
    if last:
        outs = (
            plane,
            jax.ShapeDtypeStruct((2, MODES, DET, DET), F32),
            half,
            half,
            jax.ShapeDtypeStruct((8, HALF), F32),
        )
    else:
        outs = (plane, plane, half, half)
    scratch = [
        pltpu.VMEM((2, 2 * DET + 8, DET), F32),
        pltpu.VMEM((2, DET, DET), F32),
        pltpu.VMEM((2, MODES * DET, DET), BF16),
        pltpu.VMEM((2, MODES * DET, DET), BF16),
        pltpu.VMEM((2, MODES * DET, DET), F32),
        pltpu.VMEM((2, DET, MODES * DET), BF16),
        pltpu.VMEM((2, DET, MODES * DET), BF16),
        pltpu.VMEM((2, DET, MODES * DET), F32),
    ]
    if last:
        scratch += [
            pltpu.VMEM((2, MODES * DET, DET), F32),
            pltpu.VMEM((2, DET, MODES * DET), F32),
        ]
    tables = 6 if last else 4
    scratch += [pltpu.VMEM((2, 2, DET, DET), BF16)] * tables
    scratch += [pltpu.SemaphoreType.DMA((tables,))]

    def body(*refs):
        gradient_kernel(last, rate, *refs)

    return pl.pallas_call(
        body,
        out_shape=outs,
        in_specs=[smem] * len(scalars)
        + [vmem] * len(operands)
        + [vmem, vmem, pl.BlockSpec(memory_space=pltpu.HBM)],
        out_specs=(vmem,) * len(outs),
        scratch_shapes=scratch,
        compiler_params=pltpu.CompilerParams(vmem_limit_bytes=(42 if last else 44) * 2**20),
        name="gradient_last" if last else "gradient_first",
    )(*scalars, *operands, *kept)


def plane_call(name, body, scalars, operands, outputs, weight=0):
    def kernel(*refs):
        at_scalars, refs = refs[: len(scalars)], refs[len(scalars) :]

        def strip(step, _):
            start = pl.multiple_of(step * STRIP, STRIP)
            row = lax.broadcasted_iota(jnp.int32, (STRIP, DET), 0) + start
            col = lax.broadcasted_iota(jnp.int32, (STRIP, DET), 1)
            for part in range(2):
                at = (part, pl.ds(start, STRIP), slice(None))
                values = [ref[at] for ref in refs[: len(operands)]]
                for ref, value in zip(refs[len(operands) :], body(at_scalars, row, col, *values)):
                    ref[at] = value
            return 0

        lax.fori_loop(0, DET // STRIP, strip, 0, unroll=16)

    vmem = pl.BlockSpec(memory_space=pltpu.VMEM)
    return pl.pallas_call(
        kernel,
        out_shape=[jax.ShapeDtypeStruct((2, DET, DET), F32)] * outputs,
        in_specs=[pl.BlockSpec(memory_space=pltpu.SMEM)] * len(scalars) + [vmem] * len(operands),
        out_specs=[vmem] * outputs,
        compiler_params=pltpu.CompilerParams(vmem_limit_bytes=8 * 2**20),
        name=name,
        cost_estimate=pl.CostEstimate(flops=weight, bytes_accessed=weight // 400, transcendentals=0) if weight else None,
    )(*scalars, *operands)


def side_kernel(left_at, above_at, first, second, lower, right, to_left, to_above):
    for step in range(2 * DET // STRIP):
        flat = step * STRIP
        if flat < FIRST:
            at = pl.ds(flat, STRIP)
            row = lax.broadcasted_iota(jnp.int32, (STRIP, DET), 0) + flat % DET
            to_left[at, :] = jnp.where(row >= left_at[0, 0], first[at, :], lower[at, :])
        else:
            at = pl.ds(flat - FIRST, STRIP)
            col = lax.broadcasted_iota(jnp.int32, (STRIP, DET), 1)
            to_above[at, :] = jnp.where(col >= above_at[0, 1], second[at, :], right[at, :])


def side_call(left_at, above_at, *operands):
    vmem = pl.BlockSpec(memory_space=pltpu.VMEM)
    return pl.pallas_call(
        side_kernel,
        out_shape=[jax.ShapeDtypeStruct((rows, DET), F32) for rows in (FIRST, 2 * DET - FIRST)],
        in_specs=[pl.BlockSpec(memory_space=pltpu.SMEM)] * 2 + [vmem] * 4,
        out_specs=[vmem] * 2,
        compiler_params=pltpu.CompilerParams(vmem_limit_bytes=8 * 2**20),
        name="sides",
    )(left_at, above_at, *operands)


def merge_cells(corners, row, col, own, left, right):
    here_at, left_at, right_at, above_at, below_at = corners
    inside = row < here_at[0, 0]
    inside_left = row < left_at[0, 0]
    inside_right = row < right_at[0, 0]
    near = col >= here_at[0, 1]
    left = jnp.where(col < left_at[0, 1], left, 0.0)
    right = jnp.where(col >= right_at[0, 1], right, 0.0)
    own_near = jnp.where(near, own, 0.0)
    own_far = jnp.where(near, 0.0, own)

    def gathered(wanted, start):
        near_sum = jnp.where(inside == wanted, own_near, 0.0) + jnp.where(inside_left == wanted, left, 0.0)
        far_sum = jnp.where(inside == wanted, own_far, 0.0) + jnp.where(inside_right == wanted, right, 0.0)
        return jnp.where(col >= start, near_sum, far_sum)

    merged = own + jnp.where(
        near,
        jnp.where(inside == inside_left, left, 0.0),
        jnp.where(inside == inside_right, right, 0.0),
    )
    return merged, gathered(True, below_at[0, 1]), gathered(False, above_at[0, 1])


def settle_cells(corners, row, col, own, left):
    here_at, left_at = corners
    own = jnp.where(col >= here_at[0, 1], own, 0.0)
    left = jnp.where(col < left_at[0, 1], left, 0.0)
    own_here, left_here = row >= here_at[0, 0], row >= left_at[0, 0]
    down = jnp.where(own_here, 0.0, own) + jnp.where(left_here, 0.0, left)
    stays = jnp.where(own_here, own, 0.0) + jnp.where(left_here, left, 0.0)
    return down, stays


def shifted(value, axis, steps):
    count = lax.axis_size(axis)
    initial, last = (max(0, -steps), min(count, count - steps))
    return lax.ppermute(value, axis, [(source, source + steps) for source in range(initial, last)])


def swapped(value, axis, distance):
    count = lax.axis_size(axis)
    return lax.ppermute(value, axis, [(source, source ^ distance) for source in range(count)])


def tile_parts(keep, send):
    count = lax.axis_size("tile")
    summed = keep + swapped(send, "frame", 1)
    return lax.all_to_all(summed.reshape(count, MODES * DET // count, DET), "tile", 0, 0)


def chip_sum(part):
    distance = 2
    while distance < lax.axis_size("frame"):
        part = part + swapped(part, "frame", distance)
        distance *= 2
    return part


def spread(part):
    count = lax.axis_size("tile")
    parts = jnp.broadcast_to(part[None], (count,) + part.shape)
    mine = lax.all_to_all(parts, "tile", 0, 0).reshape(MODES, DET, DET)
    return mine, swapped(mine, "frame", 1)


def per_device(object_field, probe_modes, measured, offsets, ramp_steps):
    tile_at, frame_at = lax.axis_index("tile"), lax.axis_index("frame")
    core = frame_at & 1
    place = jnp.stack(
        [
            core,
            (tile_at == lax.axis_size("tile") - 1).astype(jnp.int32),
            (frame_at == lax.axis_size("frame") - 1).astype(jnp.int32),
        ]
    )
    rate = probe_step / (lax.axis_size("tile") * lax.axis_size("frame"))
    together = lax.optimization_barrier

    flat = object_field.reshape(2 * DET, DET)
    first, second = flat[:FIRST], flat[FIRST:]
    lower = shifted(first, "tile", -1)
    right = shifted(second, "frame", -1)
    at_left = shifted(offsets, "frame", 1)
    at_above = shifted(offsets, "tile", 1)
    lower, right, at_left, at_above = together((lower, right, at_left, at_above))
    to_left, to_above = side_call(at_left, at_above, first, second, lower, right)
    to_left, to_above, corner = together((to_left, to_above, offsets))
    side = shifted(to_left, "frame", -1)
    below = shifted(to_above, "tile", -1)
    at_right = shifted(corner, "frame", -1)
    at_below = shifted(corner, "tile", -1)
    side, below, at_right, at_below = together((side, below, at_right, at_below))

    scalars = (offsets, ramp_steps, place)
    kept = (probe_modes, measured, jnp.asarray(shift_tables()))
    grad1, patch, keep1, send1 = gradient_call(
        False, rate, scalars, (first, second, lower, right, side, below), kept
    )

    grad_left = shifted(grad1, "frame", 1)
    grad_right = shifted(grad1, "frame", -1)
    parts = tile_parts(keep1, send1)
    merged, down, up = plane_call(
        "merge",
        merge_cells,
        (offsets, at_left, at_right, at_above, at_below),
        (grad1, grad_left, grad_right),
        3,
        WEIGHT,
    )
    parts, _, _, _ = together((parts, merged, down, up))
    from_above = shifted(down, "tile", 1)
    from_below = shifted(up, "tile", -1)
    part = chip_sum(jnp.sum(parts, axis=0))
    part, from_above, from_below = together((part, from_above, from_below))
    mine, other = spread(part)

    grad_total, modes_now, keep2, send2, shift_grad = gradient_call(
        True,
        rate,
        scalars,
        (patch, merged, from_above, from_below, grad1, mine, other),
        kept,
    )

    count = lax.axis_size("tile")
    planes = modes_now.reshape(2, count, MODES * DET // count, DET)
    own_part = lax.dynamic_slice(planes, (core, tile_at, 0, 0), (1, 1) + planes.shape[2:])[0, 0]

    moved = shifted(grad_total, "frame", 1)
    parts = tile_parts(keep2, send2)
    down, stays = plane_call(
        "settle", settle_cells, (offsets, at_left), (grad_total, moved), 2, WEIGHT
    )
    parts, _, _ = together((parts, down, stays))
    part = jnp.sum(parts, axis=0)
    arrived = shifted(down, "tile", 1)
    part = own_part - rate * chip_sum(part)
    part, arrived = together((part, arrived))
    object_final = object_field - object_step * (stays + arrived)

    mine, other = spread(part)
    plane = lax.broadcasted_iota(jnp.int32, (2, MODES, DET, DET), 0)
    probe_final = jnp.where(plane == core, mine[None], other[None])
    return (object_final, probe_final, shift_grad[:1, :2])


def solution(mesh):
    placed = (
        P(None, "tile", "frame"),
        P(),
        P(("tile", "frame"), None, None),
        P(("tile", "frame"), None),
        P(("tile", "frame"), None),
    )
    return jax.shard_map(
        per_device,
        mesh=mesh,
        in_specs=placed,
        out_specs=(P(None, "tile", "frame"), P(), P(("tile", "frame"), None)),
        check_vma=False,
    )
```

```python
import math

import jax
import jax.numpy as jnp
import numpy as np
from jax import lax
from jax.experimental import pallas as pl
from jax.experimental.pallas import tpu as pltpu
from jax.sharding import PartitionSpec as P

DET = 256
HALF = 128
MODES = 3
RAMPS = 8
STRIP = 16
FIRST = 384
EXTRA = 8

object_step = 0.05
probe_step = 0.5
fresnel = 0.25

WEIGHT = 2 * 10**10
VMEM_LIMIT = 18 * 2**20

F32 = jnp.float32
BF16 = jnp.bfloat16


def block_rows(eigenvalues):
    counter = np.arange(DET)
    waves = np.exp(2j * np.pi * (np.outer(counter, counter) % DET) / DET)
    column = waves @ eigenvalues / DET
    columns = [(column[:HALF] + column[HALF:]) / 2, (column[:HALF] - column[HALF:]) / 2]
    back = (-np.arange(HALF)) % HALF
    rows = [block[back] for block in columns]
    return np.stack([part for block in rows + columns for part in (block.real, block.imag)])


def shift_rows():
    counter = np.arange(DET)
    signed = np.where(counter < DET // 2, counter, counter - DET).astype(np.float64)
    chirp = -np.pi * fresnel * signed * signed / DET
    slope = -2j * np.pi * signed / DET
    factors = [np.exp(1j * chirp + slope * (step / RAMPS)) for step in range(RAMPS)]
    every = factors + [slope * factor for factor in factors] + [slope]
    return np.stack([block_rows(factor) for factor in every]).astype(np.float32)


def fill_table(rows, turned, table):
    down = lax.broadcasted_iota(jnp.int32, (HALF, HALF), 0)
    along = lax.broadcasted_iota(jnp.int32, (HALF, HALF), 1)
    ahead = along >= down if turned else down >= along
    for block in range(2):
        parts = []
        for part in range(2):
            at = 4 * turned + 2 * block + part
            whole = pltpu.roll(jnp.broadcast_to(rows[at : at + 1, :], (HALF, HALF)), 0, 1, stride=1, stride_axis=0)
            parts.append(jnp.where(ahead, whole, -whole) if block else whole)
        real, imag = parts
        left, right = (imag, -imag) if turned else (-imag, imag)
        for half, pair in enumerate(((real, left), (right, real))):
            at = pl.ds(half * HALF, HALF)
            table[block, 0, at, :], table[block, 1, at, :] = split(jnp.concatenate(pair, axis=1))


def fill_tables(ramp, vectors, turned1, plain0, turned0, plain1):
    rows0, rows1 = vectors[ramp[0, 0]], vectors[ramp[0, 1]]
    fill_table(rows1, True, turned1)
    fill_table(rows0, False, plain0)
    fill_table(rows0, True, turned0)
    fill_table(rows1, False, plain1)


def tables_call(ramp, vectors):
    vmem = pl.BlockSpec(memory_space=pltpu.VMEM)
    return pl.pallas_call(
        fill_tables,
        out_shape=[jax.ShapeDtypeStruct((2, 2, DET, DET), BF16)] * 4,
        in_specs=[pl.BlockSpec(memory_space=pltpu.SMEM), vmem],
        out_specs=[vmem] * 4,
        compiler_params=pltpu.CompilerParams(vmem_limit_bytes=VMEM_LIMIT),
        name="tables",
        cost_estimate=pl.CostEstimate(flops=WEIGHT, bytes_accessed=WEIGHT // 400, transcendentals=0),
    )(ramp, vectors)


def split(value):
    high = value.astype(BF16)
    return high, (value - high.astype(F32)).astype(BF16)


def product(left, right):
    return lax.dot_general(
        left, right, (((1,), (0,)), ((), ())), preferred_element_type=F32
    )


def gradient_kernel(last, rate, *refs):
    refs = list(refs)
    take = lambda count: [refs.pop(0) for _ in range(count)]
    corner, ramp, place = take(3)
    if last:
        patch_in, merged, from_above, from_below, grad_before = take(5)
        total_mine, total_other, keep_before, send_before = take(4)
    else:
        own_first, own_second, lower, right, side, below = take(6)
    probe, measured = take(2)
    if last:
        (vectors,) = take(1)
    else:
        turned1, plain0, turned0, plain1 = take(4)
    if last:
        grad_out, keep_out, send_out, shift_out = take(4)
    else:
        grad_out, patch_out, keep_out, send_out = take(4)
    doubled, field, high, low, result, z_high, z_low, z_result = take(8)
    if last:
        slope_result, derived_result, probe_now = take(3)
    row0, col0, core = corner[0, 0], corner[0, 1], place[0]
    if last:
        turned1, plain0, turned0, plain1, slope1, derived0 = take(6)
        fill_tables(ramp, vectors, turned1, plain0, turned0, plain1)
        fill_table(vectors[2 * RAMPS], True, slope1)
        fill_table(vectors[RAMPS + ramp[0, 0]], False, derived0)

    def build(step):
        start = step * STRIP
        rows = pl.ds(start, STRIP)
        again = pl.ds(start + DET, STRIP)
        row_at = lax.broadcasted_iota(jnp.int32, (STRIP, DET), 0) + start
        col_at = lax.broadcasted_iota(jnp.int32, (STRIP, DET), 1)
        if last:
            outside = ((row_at < row0) & (place[1] == 1)) | ((col_at < col0) & (place[2] == 1))
        for part in range(2):
            if last:
                moved = jnp.where(row_at >= row0, from_above[part, rows, :], from_below[part, rows, :])
                cells = patch_in[part, rows, :] - object_step * (merged[part, rows, :] + moved)
                cells = jnp.where(outside, 0.0, cells)
            else:
                flat = part * DET + step * STRIP
                if flat < FIRST:
                    at = pl.ds(flat, STRIP)
                    column = jnp.where(row_at >= row0, own_first[at, :], lower[at, :])
                    cells = jnp.where(col_at >= col0, column, side[at, :])
                else:
                    at = pl.ds(flat - FIRST, STRIP)
                    line = jnp.where(col_at >= col0, own_second[at, :], right[at, :])
                    cells = jnp.where(row_at >= row0, line, below[at, :])
                patch_out[part, rows, :] = cells
            doubled[part, rows, :] = cells
            doubled[part, again, :] = cells
        if last:
            for mode in range(MODES):
                mine = total_mine[mode, rows, :]
                other = total_other[mode, rows, :]
                probe_now[0, mode, rows, :] = probe[0, mode, rows, :] - rate * jnp.where(core == 0, mine, other)
                probe_now[1, mode, rows, :] = probe[1, mode, rows, :] - rate * jnp.where(core == 0, other, mine)

    for step in range(DET // STRIP):
        build(step)
    modes = probe_now if last else probe
    back = lax.rem(DET - col0, DET)

    def rows_from(part, first):
        down = lax.rem(first, 8)
        at = pl.ds(pl.multiple_of(first - down, 8), STRIP + 8)
        return pltpu.roll(doubled[part, at, :], lax.rem(STRIP + 8 - down, STRIP + 8), 0)[:STRIP]

    def enter(step, _):
        start = pl.multiple_of(step * STRIP, STRIP)
        rows = pl.ds(start, STRIP)
        real = pltpu.roll(rows_from(0, row0 + start), back, 1)
        imag = pltpu.roll(rows_from(1, row0 + start), back, 1)
        field[0, rows, :] = real
        field[1, rows, :] = imag
        for mode in range(MODES):
            probe_real = modes[0, mode, rows, :]
            probe_imag = modes[1, mode, rows, :]
            exit_real = probe_real * real - probe_imag * imag
            exit_imag = probe_real * imag + probe_imag * real
            at = pl.ds(pl.multiple_of(mode * DET + start, STRIP), STRIP)
            for block, sign in ((0, 1.0), (1, -1.0)):
                both = jnp.concatenate(
                    [
                        exit_real[:, :HALF] + sign * exit_real[:, HALF:],
                        exit_imag[:, :HALF] + sign * exit_imag[:, HALF:],
                    ],
                    axis=1,
                )
                high[block, at, :], low[block, at, :] = split(both)
        return 0

    lax.fori_loop(0, DET // STRIP, enter, 0, unroll=16)

    def times_right(block, mode, table, where):
        at = pl.ds(mode * DET, DET)
        left_high, left_low = high[block, at, :], low[block, at, :]
        where[block, at, :] = (
            product(left_high, table[block, 0])
            + product(left_low, table[block, 0])
            + product(left_high, table[block, 1])
        )

    def times_left(block, mode, table, where):
        at = pl.ds(mode * DET, DET)
        right_high, right_low = z_high[block, :, at], z_low[block, :, at]
        where[block, :, at] = (
            product(table[block, 0], right_high)
            + product(table[block, 0], right_low)
            + product(table[block, 1], right_high)
        )

    for block in range(2):
        for mode in range(MODES):
            times_right(block, mode, turned1, result)
            if last:
                times_right(block, mode, slope1, slope_result)

    def rows_to_blocks(step, _):
        start = pl.multiple_of(step * STRIP, STRIP)
        for mode in range(MODES):
            top = pl.ds(pl.multiple_of(mode * DET + start, STRIP), STRIP)
            bottom = pl.ds(pl.multiple_of(mode * DET + HALF + start, STRIP), STRIP)
            sums = [(result[col, top, :] + result[col, bottom, :]) for col in range(2)]
            gaps = [(result[col, top, :] - result[col, bottom, :]) for col in range(2)]
            for block, pair in ((0, sums), (1, gaps)):
                for part in range(2):
                    lanes = slice(part * HALF, (part + 1) * HALF)
                    both = jnp.concatenate([pair[0][:, lanes], pair[1][:, lanes]], axis=1)
                    at = pl.ds(pl.multiple_of(part * HALF + start, STRIP), STRIP)
                    cols = pl.ds(mode * DET, DET)
                    z_high[block, at, cols], z_low[block, at, cols] = split(both)
        return 0

    lax.fori_loop(0, HALF // STRIP, rows_to_blocks, 0, unroll=8)

    for block in range(2):
        for mode in range(MODES):
            times_left(block, mode, plain0, z_result)
            if last:
                times_left(block, mode, derived0, derived_result)

    def misfits(step, running):
        start = pl.multiple_of(step * STRIP, STRIP)
        low_rows = pl.ds(start, STRIP)
        high_rows = pl.ds(pl.multiple_of(start + HALF, STRIP), STRIP)

        def waves(mode, part):
            at = pl.ds(pl.multiple_of(part * HALF + start, STRIP), STRIP)
            cols = pl.ds(mode * DET, DET)
            even, odd = z_result[0, at, cols], z_result[1, at, cols]

            def spread(value):
                return jnp.concatenate(
                    [value[:, :HALF] + value[:, HALF:], value[:, :HALF] - value[:, HALF:]], axis=1
                )

            return spread(even + odd), spread(even - odd)

        top_sum = bottom_sum = None
        held = []
        for mode in range(MODES):
            for part in range(2):
                top, bottom = waves(mode, part)
                held.append((mode, part, top, bottom))
                top_sum = top * top if top_sum is None else top_sum + top * top
                bottom_sum = bottom * bottom if bottom_sum is None else bottom_sum + bottom * bottom
        top_gap = 2.0 * (top_sum - measured[0, low_rows, :])
        bottom_gap = 2.0 * (bottom_sum - measured[0, high_rows, :])

        def fold(value):
            return jnp.concatenate(
                [value[:, :HALF] + value[:, HALF:], value[:, :HALF] - value[:, HALF:]], axis=1
            )

        for mode, part, top, bottom in held:
            top_grad = fold(top_gap * top)
            bottom_grad = fold(bottom_gap * bottom)
            at = pl.ds(pl.multiple_of(part * HALF + start, STRIP), STRIP)
            cols = pl.ds(mode * DET, DET)
            for block, both in ((0, top_grad + bottom_grad), (1, top_grad - bottom_grad)):
                z_high[block, at, cols], z_low[block, at, cols] = split(both)
                if last:
                    running = running + both * derived_result[block, at, cols]
        return running

    zeros = jnp.zeros((STRIP, DET), F32) if last else 0
    slope_rows = lax.fori_loop(0, HALF // STRIP, misfits, zeros, unroll=8)

    for block in range(2):
        for mode in range(MODES):
            times_left(block, mode, turned0, z_result)

    def blocks_to_rows(step, _):
        start = pl.multiple_of(step * STRIP, STRIP)
        for mode in range(MODES):
            cols = pl.ds(mode * DET, DET)
            tops, bottoms = [], []
            for part in range(2):
                at = pl.ds(pl.multiple_of(part * HALF + start, STRIP), STRIP)
                even, odd = z_result[0, at, cols], z_result[1, at, cols]
                tops.append(even + odd)
                bottoms.append(even - odd)
            for offset, pair in ((0, tops), (HALF, bottoms)):
                at = pl.ds(pl.multiple_of(mode * DET + offset + start, STRIP), STRIP)
                for block in range(2):
                    lanes = slice(block * HALF, (block + 1) * HALF)
                    both = jnp.concatenate([pair[0][:, lanes], pair[1][:, lanes]], axis=1)
                    high[block, at, :], low[block, at, :] = split(both)
        return 0

    lax.fori_loop(0, HALF // STRIP, blocks_to_rows, 0, unroll=8)

    for block in range(2):
        for mode in range(MODES):
            times_right(block, mode, plain1, result)

    def leave(step, running):
        start = pl.multiple_of(step * STRIP, STRIP)
        rows = pl.ds(start, STRIP)
        real, imag = field[0, rows, :], field[1, rows, :]
        grad_real = jnp.zeros((STRIP, DET), F32)
        grad_imag = jnp.zeros((STRIP, DET), F32)
        for mode in range(MODES):
            at = pl.ds(pl.multiple_of(mode * DET + start, STRIP), STRIP)
            even, odd = result[0, at, :], result[1, at, :]
            if last:
                running = running + even * slope_result[0, at, :] + odd * slope_result[1, at, :]
            plus, minus = even + odd, even - odd
            exit_real = jnp.concatenate([plus[:, :HALF], minus[:, :HALF]], axis=1)
            exit_imag = jnp.concatenate([plus[:, HALF:], minus[:, HALF:]], axis=1)
            probe_real = modes[0, mode, rows, :]
            probe_imag = modes[1, mode, rows, :]
            grad_real = grad_real + probe_real * exit_real + probe_imag * exit_imag
            grad_imag = grad_imag + probe_real * exit_imag - probe_imag * exit_real
            mode_real = real * exit_real + imag * exit_imag
            mode_imag = real * exit_imag - imag * exit_real
            keep = jnp.where(core == 0, mode_real, mode_imag)
            send = jnp.where(core == 0, mode_imag, mode_real)
            if last:
                keep = keep + keep_before[mode, rows, :]
                send = send + send_before[mode, rows, :]
            keep_out[mode, rows, :] = keep
            send_out[mode, rows, :] = send
        again = pl.ds(pl.multiple_of(start + DET, STRIP), STRIP)
        for part, value in ((0, grad_real), (1, grad_imag)):
            turned = pltpu.roll(value, col0, 1)
            doubled[part, rows, :] = turned
            doubled[part, again, :] = turned
        return running

    slope_cols = lax.fori_loop(0, DET // STRIP, leave, zeros, unroll=16)

    def wrap(step, _):
        start = pl.multiple_of(step * STRIP, STRIP)
        rows = pl.ds(start, STRIP)
        for part in range(2):
            value = rows_from(part, DET - row0 + start)
            at = pl.ds(pl.multiple_of(part * DET + start, STRIP), STRIP)
            if last:
                grad_out[part, rows, :] = value + grad_before[at, :]
            else:
                grad_out[at, :] = value
        return 0

    lax.fori_loop(0, DET // STRIP, wrap, 0, unroll=16)

    if last:
        lane = lax.broadcasted_iota(jnp.int32, (1, 2), 1)
        shift_out[...] = jnp.where(lane == 0, jnp.sum(slope_rows), 2.0 * jnp.sum(slope_cols)) / DET
    else:
        grad_out[pl.ds(2 * DET, EXTRA), :] = corner_rows(row0, col0)


def corner_rows(row0, col0):
    lane = lax.broadcasted_iota(jnp.int32, (EXTRA, DET), 1)
    return jnp.where(lane == 0, row0.astype(F32), jnp.where(lane == 1, col0.astype(F32), 0.0))


def corner_of(ref, at):
    row = ref[pl.ds(at, EXTRA), :]
    return row[:1, :1], row[:1, 1:2]


def gradient_call(last, rate, scalars, operands, kept):
    plane = jax.ShapeDtypeStruct((2, DET, DET), F32)
    half = jax.ShapeDtypeStruct((MODES, DET, DET), F32)
    vmem = pl.BlockSpec(memory_space=pltpu.VMEM)
    smem = pl.BlockSpec(memory_space=pltpu.SMEM)
    if last:
        outs = (plane, half, half, jax.ShapeDtypeStruct((1, 2), F32))
    else:
        outs = (jax.ShapeDtypeStruct((2 * DET + EXTRA, DET), F32), plane, half, half)
    scratch = [
        pltpu.VMEM((2, 2 * DET + 8, DET), F32),
        pltpu.VMEM((2, DET, DET), F32),
        pltpu.VMEM((2, MODES * DET, DET), BF16),
        pltpu.VMEM((2, MODES * DET, DET), BF16),
        pltpu.VMEM((2, MODES * DET, DET), F32),
        pltpu.VMEM((2, DET, MODES * DET), BF16),
        pltpu.VMEM((2, DET, MODES * DET), BF16),
        pltpu.VMEM((2, DET, MODES * DET), F32),
    ]
    if last:
        scratch += [
            pltpu.VMEM((2, MODES * DET, DET), F32),
            pltpu.VMEM((2, DET, MODES * DET), F32),
            pltpu.VMEM((2, MODES, DET, DET), F32),
        ]
    if last:
        scratch += [pltpu.VMEM((2, 2, DET, DET), BF16)] * 6

    def body(*refs):
        gradient_kernel(last, rate, *refs)

    return pl.pallas_call(
        body,
        out_shape=outs,
        in_specs=[smem] * len(scalars)
        + [vmem] * len(operands)
        + [vmem] * len(kept),
        out_specs=(vmem,) * len(outs),
        scratch_shapes=scratch,
        compiler_params=pltpu.CompilerParams(vmem_limit_bytes=VMEM_LIMIT),
        name="gradient_last" if last else "gradient_first",
    )(*scalars, *operands, *kept)


def plane_call(name, body, scalars, operands, outputs, weight=0):
    def kernel(*refs):
        at_scalars, refs = refs[: len(scalars)], refs[len(scalars) :]

        def strip(step, _):
            start = pl.multiple_of(step * STRIP, STRIP)
            row = lax.broadcasted_iota(jnp.int32, (STRIP, DET), 0) + start
            col = lax.broadcasted_iota(jnp.int32, (STRIP, DET), 1)
            for part in range(2):
                at = (part, pl.ds(start, STRIP), slice(None))
                values = [ref[at] for ref in refs[: len(operands)]]
                for ref, value in zip(refs[len(operands) :], body(at_scalars, row, col, *values)):
                    ref[at] = value
            return 0

        lax.fori_loop(0, DET // STRIP, strip, 0, unroll=16)

    vmem = pl.BlockSpec(memory_space=pltpu.VMEM)
    return pl.pallas_call(
        kernel,
        out_shape=[jax.ShapeDtypeStruct((2, DET, DET), F32)] * outputs,
        in_specs=[pl.BlockSpec(memory_space=pltpu.SMEM)] * len(scalars) + [vmem] * len(operands),
        out_specs=[vmem] * outputs,
        compiler_params=pltpu.CompilerParams(vmem_limit_bytes=VMEM_LIMIT),
        name=name,
        cost_estimate=pl.CostEstimate(flops=weight, bytes_accessed=weight // 400, transcendentals=0) if weight else None,
    )(*scalars, *operands)


def side_kernel(here_at, left_at, above_at, first, second, lower, right, to_left, to_above):
    for step in range(2 * DET // STRIP):
        flat = step * STRIP
        if flat < FIRST:
            at = pl.ds(flat, STRIP)
            row = lax.broadcasted_iota(jnp.int32, (STRIP, DET), 0) + flat % DET
            to_left[at, :] = jnp.where(row >= left_at[0, 0], first[at, :], lower[at, :])
        else:
            at = pl.ds(flat - FIRST, STRIP)
            col = lax.broadcasted_iota(jnp.int32, (STRIP, DET), 1)
            to_above[at, :] = jnp.where(col >= above_at[0, 1], second[at, :], right[at, :])
    to_above[pl.ds(2 * DET - FIRST, EXTRA), :] = corner_rows(here_at[0, 0], here_at[0, 1])


def side_call(here_at, left_at, above_at, *operands):
    vmem = pl.BlockSpec(memory_space=pltpu.VMEM)
    return pl.pallas_call(
        side_kernel,
        out_shape=[jax.ShapeDtypeStruct((rows, DET), F32) for rows in (FIRST, 2 * DET - FIRST + EXTRA)],
        in_specs=[pl.BlockSpec(memory_space=pltpu.SMEM)] * 3 + [vmem] * 4,
        out_specs=[vmem] * 2,
        compiler_params=pltpu.CompilerParams(vmem_limit_bytes=VMEM_LIMIT),
        name="sides",
    )(here_at, left_at, above_at, *operands)


def merge_kernel(here_at, above_at, own_ref, left_ref, right_ref, below_ref, merged, down, up):
    left_row, left_col = corner_of(left_ref, 2 * DET)
    right_row, right_col = corner_of(right_ref, 2 * DET)
    _, below_col = corner_of(below_ref, 2 * DET - FIRST)
    above_col = above_at[0, 1].astype(F32)

    def strip(step, _):
        start = pl.multiple_of(step * STRIP, STRIP)
        row = lax.broadcasted_iota(jnp.int32, (STRIP, DET), 0) + start
        col = lax.broadcasted_iota(jnp.int32, (STRIP, DET), 1)
        for part in range(2):
            flat = pl.ds(pl.multiple_of(part * DET + start, STRIP), STRIP)
            values = merge_cells(
                row.astype(F32),
                col.astype(F32),
                (here_at[0, 0].astype(F32), here_at[0, 1].astype(F32)),
                (left_row, left_col),
                (right_row, right_col),
                (below_col, above_col),
                *(ref[flat, :] for ref in (own_ref, left_ref, right_ref)),
            )
            for ref, value in zip((merged, down, up), values):
                ref[part, pl.ds(start, STRIP), :] = value
        return 0

    lax.fori_loop(0, DET // STRIP, strip, 0, unroll=16)


def merge_call(here_at, above_at, *operands):
    vmem = pl.BlockSpec(memory_space=pltpu.VMEM)
    return pl.pallas_call(
        merge_kernel,
        out_shape=[jax.ShapeDtypeStruct((2, DET, DET), F32)] * 3,
        in_specs=[pl.BlockSpec(memory_space=pltpu.SMEM)] * 2 + [vmem] * 4,
        out_specs=[vmem] * 3,
        compiler_params=pltpu.CompilerParams(vmem_limit_bytes=VMEM_LIMIT),
        name="merge",
        cost_estimate=pl.CostEstimate(flops=WEIGHT, bytes_accessed=WEIGHT // 400, transcendentals=0),
    )(here_at, above_at, *operands)


def merge_cells(row, col, here_at, left_at, right_at, starts, own, left, right):
    below_start, above_start = starts
    inside = row < here_at[0]
    inside_left = row < left_at[0]
    inside_right = row < right_at[0]
    near = col >= here_at[1]
    left = jnp.where(col < left_at[1], left, 0.0)
    right = jnp.where(col >= right_at[1], right, 0.0)
    own_near = jnp.where(near, own, 0.0)
    own_far = jnp.where(near, 0.0, own)

    def gathered(wanted, start):
        kept = (lambda at, value: jnp.where(at, value, 0.0)) if wanted else (lambda at, value: jnp.where(at, 0.0, value))
        near_sum = kept(inside, own_near) + kept(inside_left, left)
        far_sum = kept(inside, own_far) + kept(inside_right, right)
        return jnp.where(col >= start, near_sum, far_sum)

    merged = own + jnp.where(
        near,
        jnp.where(inside ^ inside_left, 0.0, left),
        jnp.where(inside ^ inside_right, 0.0, right),
    )
    return merged, gathered(True, below_start), gathered(False, above_start)


def settle_cells(corners, row, col, own, left):
    here_at, left_at = corners
    own = jnp.where(col >= here_at[0, 1], own, 0.0)
    left = jnp.where(col < left_at[0, 1], left, 0.0)
    own_here, left_here = row >= here_at[0, 0], row >= left_at[0, 0]
    down = jnp.where(own_here, 0.0, own) + jnp.where(left_here, 0.0, left)
    stays = jnp.where(own_here, own, 0.0) + jnp.where(left_here, left, 0.0)
    return down, stays


def shifted(value, axis, steps):
    count = lax.axis_size(axis)
    initial, last = (max(0, -steps), min(count, count - steps))
    return lax.ppermute(value, axis, [(source, source + steps) for source in range(initial, last)])


def swapped(value, axis, distance):
    count = lax.axis_size(axis)
    return lax.ppermute(value, axis, [(source, source ^ distance) for source in range(count)])


def tile_parts(keep, send):
    count = lax.axis_size("tile")
    summed = keep + swapped(send, "frame", 1)
    return lax.all_to_all(summed.reshape(count, MODES * DET // count, DET), "tile", 0, 0)


def chip_sum(part):
    distance = 2
    while distance < lax.axis_size("frame"):
        part = part + swapped(part, "frame", distance)
        distance *= 2
    return part


def quick_chip_sum(part):
    if lax.axis_size("frame") != 16:
        return chip_sum(part)
    for pairs in (
        ((0, 1), (2, 3), (4, 5), (6, 7)),
        ((1, 2), (3, 4), (5, 6), (7, 0)),
        ((1, 6), (2, 5), (3, 0), (4, 7)),
    ):
        ways = [way for one, other in pairs for way in ((one, other), (other, one))]
        moves = [(2 * one + core, 2 * other + core) for one, other in ways for core in range(2)]
        part = part + lax.ppermute(part, "frame", moves)
    return part


def spread(part):
    count = lax.axis_size("tile")
    parts = jnp.broadcast_to(part[None], (count,) + part.shape)
    mine = lax.all_to_all(parts, "tile", 0, 0).reshape(MODES, DET, DET)
    return mine, swapped(mine, "frame", 1)


def per_device(object_field, probe_modes, measured, offsets, ramp_steps):
    tile_at, frame_at = lax.axis_index("tile"), lax.axis_index("frame")
    core = frame_at & 1
    place = jnp.stack(
        [
            core,
            (tile_at == lax.axis_size("tile") - 1).astype(jnp.int32),
            (frame_at == lax.axis_size("frame") - 1).astype(jnp.int32),
        ]
    )
    rate = probe_step / (lax.axis_size("tile") * lax.axis_size("frame"))
    together = lax.optimization_barrier

    flat = object_field.reshape(2 * DET, DET)
    first, second = flat[:FIRST], flat[FIRST:]
    lower = shifted(first, "tile", -1)
    right = shifted(second, "frame", -1)
    at_left = shifted(offsets, "frame", 1)
    at_above = shifted(offsets, "tile", 1)
    lower, right, at_left, at_above = together((lower, right, at_left, at_above))
    to_left, to_above = side_call(offsets, at_left, at_above, first, second, lower, right)
    side = shifted(to_left, "frame", -1)
    below = shifted(to_above, "tile", -1)

    ramp, _, _ = together((ramp_steps, to_left, to_above))
    vectors = jnp.asarray(shift_rows())
    side, below, *filled = together((side, below, *tables_call(ramp, vectors)))

    scalars = (offsets, ramp_steps, place)
    kept = (probe_modes, measured)
    grad1, patch, keep1, send1 = gradient_call(
        False, rate, scalars, (first, second, lower, right, side, below), kept + tuple(filled)
    )

    grad_left = shifted(grad1, "frame", 1)
    grad_right = shifted(grad1, "frame", -1)
    parts = tile_parts(keep1, send1)
    merged, down, up = merge_call(offsets, at_above, grad1, grad_left, grad_right, below)
    parts, _, _, _ = together((parts, merged, down, up))
    from_above = shifted(down, "tile", 1)
    from_below = shifted(up, "tile", -1)
    part = quick_chip_sum(jnp.sum(parts, axis=0))
    part, from_above, from_below = together((part, from_above, from_below))
    mine, other = spread(part)

    grad_total, keep2, send2, shift_grad = gradient_call(
        True,
        rate,
        scalars,
        (patch, merged, from_above, from_below, grad1, mine, other, keep1, send1),
        kept + (vectors,),
    )

    count = lax.axis_size("tile")
    planes = probe_modes.reshape(2, count, MODES * DET // count, DET)
    own_part = lax.dynamic_slice(planes, (core, tile_at, 0, 0), (1, 1) + planes.shape[2:])[0, 0]

    moved = shifted(grad_total, "frame", 1)
    parts = tile_parts(keep2, send2)
    down, stays = plane_call(
        "settle", settle_cells, (offsets, at_left), (grad_total, moved), 2, WEIGHT
    )
    parts, _, _ = together((parts, down, stays))
    part = jnp.sum(parts, axis=0)
    arrived = shifted(down, "tile", 1)
    part = own_part - rate * chip_sum(part)
    part, arrived = together((part, arrived))
    object_final = object_field - object_step * (stays + arrived)

    mine, other = spread(part)
    plane = lax.broadcasted_iota(jnp.int32, (2, MODES, DET, DET), 0)
    probe_final = jnp.where(plane == core, mine[None], other[None])
    return (object_final, probe_final, shift_grad)


def solution(mesh):
    placed = (
        P(None, "tile", "frame"),
        P(),
        P(("tile", "frame"), None, None),
        P(("tile", "frame"), None),
        P(("tile", "frame"), None),
    )
    return jax.shard_map(
        per_device,
        mesh=mesh,
        in_specs=placed,
        out_specs=(P(None, "tile", "frame"), P(), P(("tile", "frame"), None)),
        check_vma=False,
    )
```

```python
import math

import jax
import jax.numpy as jnp
import numpy as np
from jax import lax
from jax.experimental import pallas as pl
from jax.experimental.pallas import tpu as pltpu
from jax.sharding import PartitionSpec as P

DET = 256
HALF = 128
MODES = 3
RAMPS = 8
STRIP = 16
FIRST = 384
EXTRA = 8

object_step = 0.05
probe_step = 0.5
fresnel = 0.25

WEIGHT = 2 * 10**10
VMEM_LIMIT = 18 * 2**20

F32 = jnp.float32
BF16 = jnp.bfloat16


def block_rows(eigenvalues):
    counter = np.arange(DET)
    waves = np.exp(2j * np.pi * (np.outer(counter, counter) % DET) / DET)
    column = waves @ eigenvalues / DET
    columns = [(column[:HALF] + column[HALF:]) / 2, (column[:HALF] - column[HALF:]) / 2]
    back = (-np.arange(HALF)) % HALF
    rows = [block[back] for block in columns]
    return np.stack([part for block in rows + columns for part in (block.real, block.imag)])


def shift_rows():
    counter = np.arange(DET)
    signed = np.where(counter < DET // 2, counter, counter - DET).astype(np.float64)
    chirp = -np.pi * fresnel * signed * signed / DET
    slope = -2j * np.pi * signed / DET
    factors = [np.exp(1j * chirp + slope * (step / RAMPS)) for step in range(RAMPS)]
    every = factors + [slope * factor for factor in factors] + [slope]
    return np.stack([block_rows(factor) for factor in every]).astype(np.float32)


def fill_table(rows, turned, table):
    down = lax.broadcasted_iota(jnp.int32, (HALF, HALF), 0)
    along = lax.broadcasted_iota(jnp.int32, (HALF, HALF), 1)
    ahead = along >= down if turned else down >= along
    for block in range(2):
        parts = []
        for part in range(2):
            at = 4 * turned + 2 * block + part
            whole = pltpu.roll(jnp.broadcast_to(rows[at : at + 1, :], (HALF, HALF)), 0, 1, stride=1, stride_axis=0)
            parts.append(jnp.where(ahead, whole, -whole) if block else whole)
        real, imag = parts
        left, right = (imag, -imag) if turned else (-imag, imag)
        for half, pair in enumerate(((real, left), (right, real))):
            at = pl.ds(half * HALF, HALF)
            table[block, 0, at, :], table[block, 1, at, :] = split(jnp.concatenate(pair, axis=1))


def fill_tables(ramp, vectors, turned1, plain0, turned0, plain1):
    rows0, rows1 = vectors[ramp[0, 0]], vectors[ramp[0, 1]]
    fill_table(rows1, True, turned1)
    fill_table(rows0, False, plain0)
    fill_table(rows0, True, turned0)
    fill_table(rows1, False, plain1)


def tables_call(ramp, vectors):
    vmem = pl.BlockSpec(memory_space=pltpu.VMEM)
    return pl.pallas_call(
        fill_tables,
        out_shape=[jax.ShapeDtypeStruct((2, 2, DET, DET), BF16)] * 4,
        in_specs=[pl.BlockSpec(memory_space=pltpu.SMEM), vmem],
        out_specs=[vmem] * 4,
        compiler_params=pltpu.CompilerParams(vmem_limit_bytes=VMEM_LIMIT),
        name="tables",
        cost_estimate=pl.CostEstimate(flops=WEIGHT, bytes_accessed=WEIGHT // 400, transcendentals=0),
    )(ramp, vectors)


def split(value):
    high = value.astype(BF16)
    return high, (value - high.astype(F32)).astype(BF16)


def product(left, right):
    return lax.dot_general(
        left, right, (((1,), (0,)), ((), ())), preferred_element_type=F32
    )


def gradient_kernel(last, rate, *refs):
    refs = list(refs)
    take = lambda count: [refs.pop(0) for _ in range(count)]
    corner, ramp, place = take(3)
    if last:
        patch_in, merged, from_above, from_below, grad_before = take(5)
        total_mine, total_other, keep_before, send_before = take(4)
    else:
        own_first, own_second, lower, right, side, below = take(6)
    probe, measured = take(2)
    if last:
        (vectors,) = take(1)
    else:
        turned1, plain0, turned0, plain1 = take(4)
    if last:
        grad_out, keep_out, send_out, shift_out = take(4)
    else:
        grad_out, patch_out, keep_out, send_out = take(4)
    doubled, field, high, low, result, z_high, z_low, z_result = take(8)
    if last:
        slope_result, derived_result, probe_now = take(3)
    row0, col0, core = corner[0, 0], corner[0, 1], place[0]
    if last:
        turned1, plain0, turned0, plain1, slope1, derived0 = take(6)
        fill_tables(ramp, vectors, turned1, plain0, turned0, plain1)
        fill_table(vectors[2 * RAMPS], True, slope1)
        fill_table(vectors[RAMPS + ramp[0, 0]], False, derived0)

    def build(step):
        start = step * STRIP
        rows = pl.ds(start, STRIP)
        again = pl.ds(start + DET, STRIP)
        row_at = lax.broadcasted_iota(jnp.int32, (STRIP, DET), 0) + start
        col_at = lax.broadcasted_iota(jnp.int32, (STRIP, DET), 1)
        if last:
            outside = ((row_at < row0) & (place[1] == 1)) | ((col_at < col0) & (place[2] == 1))
        for part in range(2):
            if last:
                moved = jnp.where(row_at >= row0, from_above[part, rows, :], from_below[part, rows, :])
                cells = patch_in[part, rows, :] - object_step * (merged[part, rows, :] + moved)
                cells = jnp.where(outside, 0.0, cells)
            else:
                flat = part * DET + step * STRIP
                if flat < FIRST:
                    at = pl.ds(flat, STRIP)
                    column = jnp.where(row_at >= row0, own_first[at, :], lower[at, :])
                    cells = jnp.where(col_at >= col0, column, side[at, :])
                else:
                    at = pl.ds(flat - FIRST, STRIP)
                    line = jnp.where(col_at >= col0, own_second[at, :], right[at, :])
                    cells = jnp.where(row_at >= row0, line, below[at, :])
                patch_out[part, rows, :] = cells
            doubled[part, rows, :] = cells
            doubled[part, again, :] = cells
        if last:
            for mode in range(MODES):
                mine = total_mine[mode, rows, :]
                other = total_other[mode, rows, :]
                probe_now[0, mode, rows, :] = probe[0, mode, rows, :] - rate * jnp.where(core == 0, mine, other)
                probe_now[1, mode, rows, :] = probe[1, mode, rows, :] - rate * jnp.where(core == 0, other, mine)

    for step in range(DET // STRIP):
        build(step)
    modes = probe_now if last else probe
    back = lax.rem(DET - col0, DET)

    def rows_from(part, first):
        down = lax.rem(first, 8)
        at = pl.ds(pl.multiple_of(first - down, 8), STRIP + 8)
        return pltpu.roll(doubled[part, at, :], lax.rem(STRIP + 8 - down, STRIP + 8), 0)[:STRIP]

    def enter(step, _):
        start = pl.multiple_of(step * STRIP, STRIP)
        rows = pl.ds(start, STRIP)
        real = pltpu.roll(rows_from(0, row0 + start), back, 1)
        imag = pltpu.roll(rows_from(1, row0 + start), back, 1)
        field[0, rows, :] = real
        field[1, rows, :] = imag
        for mode in range(MODES):
            probe_real = modes[0, mode, rows, :]
            probe_imag = modes[1, mode, rows, :]
            exit_real = probe_real * real - probe_imag * imag
            exit_imag = probe_real * imag + probe_imag * real
            at = pl.ds(pl.multiple_of(mode * DET + start, STRIP), STRIP)
            for block, sign in ((0, 1.0), (1, -1.0)):
                both = jnp.concatenate(
                    [
                        exit_real[:, :HALF] + sign * exit_real[:, HALF:],
                        exit_imag[:, :HALF] + sign * exit_imag[:, HALF:],
                    ],
                    axis=1,
                )
                high[block, at, :], low[block, at, :] = split(both)
        return 0

    lax.fori_loop(0, DET // STRIP, enter, 0, unroll=16)

    def times_right(block, mode, table, where):
        at = pl.ds(mode * DET, DET)
        left_high, left_low = high[block, at, :], low[block, at, :]
        where[block, at, :] = (
            product(left_high, table[block, 0])
            + product(left_low, table[block, 0])
            + product(left_high, table[block, 1])
        )

    def times_left(block, mode, table, where):
        at = pl.ds(mode * DET, DET)
        right_high, right_low = z_high[block, :, at], z_low[block, :, at]
        where[block, :, at] = (
            product(table[block, 0], right_high)
            + product(table[block, 0], right_low)
            + product(table[block, 1], right_high)
        )

    for block in range(2):
        for mode in range(MODES):
            times_right(block, mode, turned1, result)
            if last:
                times_right(block, mode, slope1, slope_result)

    def rows_to_blocks(step, _):
        start = pl.multiple_of(step * STRIP, STRIP)
        for mode in range(MODES):
            top = pl.ds(pl.multiple_of(mode * DET + start, STRIP), STRIP)
            bottom = pl.ds(pl.multiple_of(mode * DET + HALF + start, STRIP), STRIP)
            sums = [(result[col, top, :] + result[col, bottom, :]) for col in range(2)]
            gaps = [(result[col, top, :] - result[col, bottom, :]) for col in range(2)]
            for block, pair in ((0, sums), (1, gaps)):
                for part in range(2):
                    lanes = slice(part * HALF, (part + 1) * HALF)
                    both = jnp.concatenate([pair[0][:, lanes], pair[1][:, lanes]], axis=1)
                    at = pl.ds(pl.multiple_of(part * HALF + start, STRIP), STRIP)
                    cols = pl.ds(mode * DET, DET)
                    z_high[block, at, cols], z_low[block, at, cols] = split(both)
        return 0

    lax.fori_loop(0, HALF // STRIP, rows_to_blocks, 0, unroll=8)

    for block in range(2):
        for mode in range(MODES):
            times_left(block, mode, plain0, z_result)
            if last:
                times_left(block, mode, derived0, derived_result)

    def misfits(step, running):
        start = pl.multiple_of(step * STRIP, STRIP)
        low_rows = pl.ds(start, STRIP)
        high_rows = pl.ds(pl.multiple_of(start + HALF, STRIP), STRIP)

        def waves(mode, part):
            at = pl.ds(pl.multiple_of(part * HALF + start, STRIP), STRIP)
            cols = pl.ds(mode * DET, DET)
            even, odd = z_result[0, at, cols], z_result[1, at, cols]

            def spread(value):
                return jnp.concatenate(
                    [value[:, :HALF] + value[:, HALF:], value[:, :HALF] - value[:, HALF:]], axis=1
                )

            return spread(even + odd), spread(even - odd)

        top_sum = bottom_sum = None
        held = []
        for mode in range(MODES):
            for part in range(2):
                top, bottom = waves(mode, part)
                held.append((mode, part, top, bottom))
                top_sum = top * top if top_sum is None else top_sum + top * top
                bottom_sum = bottom * bottom if bottom_sum is None else bottom_sum + bottom * bottom
        top_gap = 2.0 * (top_sum - measured[0, low_rows, :])
        bottom_gap = 2.0 * (bottom_sum - measured[0, high_rows, :])

        def fold(value):
            return jnp.concatenate(
                [value[:, :HALF] + value[:, HALF:], value[:, :HALF] - value[:, HALF:]], axis=1
            )

        for mode, part, top, bottom in held:
            top_grad = fold(top_gap * top)
            bottom_grad = fold(bottom_gap * bottom)
            at = pl.ds(pl.multiple_of(part * HALF + start, STRIP), STRIP)
            cols = pl.ds(mode * DET, DET)
            for block, both in ((0, top_grad + bottom_grad), (1, top_grad - bottom_grad)):
                z_high[block, at, cols], z_low[block, at, cols] = split(both)
                if last:
                    running = running + both * derived_result[block, at, cols]
        return running

    zeros = jnp.zeros((STRIP, DET), F32) if last else 0
    slope_rows = lax.fori_loop(0, HALF // STRIP, misfits, zeros, unroll=8)

    for block in range(2):
        for mode in range(MODES):
            times_left(block, mode, turned0, z_result)

    def blocks_to_rows(step, _):
        start = pl.multiple_of(step * STRIP, STRIP)
        for mode in range(MODES):
            cols = pl.ds(mode * DET, DET)
            tops, bottoms = [], []
            for part in range(2):
                at = pl.ds(pl.multiple_of(part * HALF + start, STRIP), STRIP)
                even, odd = z_result[0, at, cols], z_result[1, at, cols]
                tops.append(even + odd)
                bottoms.append(even - odd)
            for offset, pair in ((0, tops), (HALF, bottoms)):
                at = pl.ds(pl.multiple_of(mode * DET + offset + start, STRIP), STRIP)
                for block in range(2):
                    lanes = slice(block * HALF, (block + 1) * HALF)
                    both = jnp.concatenate([pair[0][:, lanes], pair[1][:, lanes]], axis=1)
                    high[block, at, :], low[block, at, :] = split(both)
        return 0

    lax.fori_loop(0, HALF // STRIP, blocks_to_rows, 0, unroll=8)

    for block in range(2):
        for mode in range(MODES):
            times_right(block, mode, plain1, result)

    def leave(step, running):
        start = pl.multiple_of(step * STRIP, STRIP)
        rows = pl.ds(start, STRIP)
        real, imag = field[0, rows, :], field[1, rows, :]
        grad_real = jnp.zeros((STRIP, DET), F32)
        grad_imag = jnp.zeros((STRIP, DET), F32)
        for mode in range(MODES):
            at = pl.ds(pl.multiple_of(mode * DET + start, STRIP), STRIP)
            even, odd = result[0, at, :], result[1, at, :]
            if last:
                running = running + even * slope_result[0, at, :] + odd * slope_result[1, at, :]
            plus, minus = even + odd, even - odd
            exit_real = jnp.concatenate([plus[:, :HALF], minus[:, :HALF]], axis=1)
            exit_imag = jnp.concatenate([plus[:, HALF:], minus[:, HALF:]], axis=1)
            probe_real = modes[0, mode, rows, :]
            probe_imag = modes[1, mode, rows, :]
            grad_real = grad_real + probe_real * exit_real + probe_imag * exit_imag
            grad_imag = grad_imag + probe_real * exit_imag - probe_imag * exit_real
            mode_real = real * exit_real + imag * exit_imag
            mode_imag = real * exit_imag - imag * exit_real
            keep = jnp.where(core == 0, mode_real, mode_imag)
            send = jnp.where(core == 0, mode_imag, mode_real)
            if last:
                keep = keep + keep_before[mode, rows, :]
                send = send + send_before[mode, rows, :]
            keep_out[mode, rows, :] = keep
            send_out[mode, rows, :] = send
        again = pl.ds(pl.multiple_of(start + DET, STRIP), STRIP)
        for part, value in ((0, grad_real), (1, grad_imag)):
            turned = pltpu.roll(value, col0, 1)
            doubled[part, rows, :] = turned
            doubled[part, again, :] = turned
        return running

    slope_cols = lax.fori_loop(0, DET // STRIP, leave, zeros, unroll=16)

    def wrap(step, _):
        start = pl.multiple_of(step * STRIP, STRIP)
        rows = pl.ds(start, STRIP)
        for part in range(2):
            value = rows_from(part, DET - row0 + start)
            at = pl.ds(pl.multiple_of(part * DET + start, STRIP), STRIP)
            if last:
                grad_out[part, rows, :] = value + grad_before[at, :]
            else:
                grad_out[at, :] = value
        return 0

    lax.fori_loop(0, DET // STRIP, wrap, 0, unroll=16)

    if last:
        lane = lax.broadcasted_iota(jnp.int32, (1, 2), 1)
        shift_out[...] = jnp.where(lane == 0, jnp.sum(slope_rows), 2.0 * jnp.sum(slope_cols)) / DET
    else:
        grad_out[pl.ds(2 * DET, EXTRA), :] = corner_rows(row0, col0)


def corner_rows(row0, col0):
    lane = lax.broadcasted_iota(jnp.int32, (EXTRA, DET), 1)
    return jnp.where(lane == 0, row0.astype(F32), jnp.where(lane == 1, col0.astype(F32), 0.0))


def corner_of(ref, at):
    row = ref[pl.ds(at, EXTRA), :]
    return row[:1, :1], row[:1, 1:2]


def gradient_call(last, rate, scalars, operands, kept):
    plane = jax.ShapeDtypeStruct((2, DET, DET), F32)
    half = jax.ShapeDtypeStruct((MODES, DET, DET), F32)
    vmem = pl.BlockSpec(memory_space=pltpu.VMEM)
    smem = pl.BlockSpec(memory_space=pltpu.SMEM)
    if last:
        outs = (plane, half, half, jax.ShapeDtypeStruct((1, 2), F32))
    else:
        outs = (jax.ShapeDtypeStruct((2 * DET + EXTRA, DET), F32), plane, half, half)
    scratch = [
        pltpu.VMEM((2, 2 * DET + 8, DET), F32),
        pltpu.VMEM((2, DET, DET), F32),
        pltpu.VMEM((2, MODES * DET, DET), BF16),
        pltpu.VMEM((2, MODES * DET, DET), BF16),
        pltpu.VMEM((2, MODES * DET, DET), F32),
        pltpu.VMEM((2, DET, MODES * DET), BF16),
        pltpu.VMEM((2, DET, MODES * DET), BF16),
        pltpu.VMEM((2, DET, MODES * DET), F32),
    ]
    if last:
        scratch += [
            pltpu.VMEM((2, MODES * DET, DET), F32),
            pltpu.VMEM((2, DET, MODES * DET), F32),
            pltpu.VMEM((2, MODES, DET, DET), F32),
        ]
    if last:
        scratch += [pltpu.VMEM((2, 2, DET, DET), BF16)] * 6

    def body(*refs):
        gradient_kernel(last, rate, *refs)

    return pl.pallas_call(
        body,
        out_shape=outs,
        in_specs=[smem] * len(scalars)
        + [vmem] * len(operands)
        + [vmem] * len(kept),
        out_specs=(vmem,) * len(outs),
        scratch_shapes=scratch,
        compiler_params=pltpu.CompilerParams(vmem_limit_bytes=VMEM_LIMIT),
        name="gradient_last" if last else "gradient_first",
    )(*scalars, *operands, *kept)


def plane_call(name, body, scalars, operands, outputs, weight=0):
    def kernel(*refs):
        at_scalars, refs = refs[: len(scalars)], refs[len(scalars) :]

        def strip(step, _):
            start = pl.multiple_of(step * STRIP, STRIP)
            row = lax.broadcasted_iota(jnp.int32, (STRIP, DET), 0) + start
            col = lax.broadcasted_iota(jnp.int32, (STRIP, DET), 1)
            for part in range(2):
                at = (part, pl.ds(start, STRIP), slice(None))
                values = [ref[at] for ref in refs[: len(operands)]]
                for ref, value in zip(refs[len(operands) :], body(at_scalars, row, col, *values)):
                    ref[at] = value
            return 0

        lax.fori_loop(0, DET // STRIP, strip, 0, unroll=4)

    vmem = pl.BlockSpec(memory_space=pltpu.VMEM)
    return pl.pallas_call(
        kernel,
        out_shape=[jax.ShapeDtypeStruct((2, DET, DET), F32)] * outputs,
        in_specs=[pl.BlockSpec(memory_space=pltpu.SMEM)] * len(scalars) + [vmem] * len(operands),
        out_specs=[vmem] * outputs,
        compiler_params=pltpu.CompilerParams(vmem_limit_bytes=VMEM_LIMIT),
        name=name,
        cost_estimate=pl.CostEstimate(flops=weight, bytes_accessed=weight // 400, transcendentals=0) if weight else None,
    )(*scalars, *operands)


def side_kernel(here_at, left_at, above_at, first, second, lower, right, to_left, to_above):
    for step in range(2 * DET // STRIP):
        flat = step * STRIP
        if flat < FIRST:
            at = pl.ds(flat, STRIP)
            row = lax.broadcasted_iota(jnp.int32, (STRIP, DET), 0) + flat % DET
            to_left[at, :] = jnp.where(row >= left_at[0, 0], first[at, :], lower[at, :])
        else:
            at = pl.ds(flat - FIRST, STRIP)
            col = lax.broadcasted_iota(jnp.int32, (STRIP, DET), 1)
            to_above[at, :] = jnp.where(col >= above_at[0, 1], second[at, :], right[at, :])
    to_above[pl.ds(2 * DET - FIRST, EXTRA), :] = corner_rows(here_at[0, 0], here_at[0, 1])


def side_call(here_at, left_at, above_at, *operands):
    vmem = pl.BlockSpec(memory_space=pltpu.VMEM)
    return pl.pallas_call(
        side_kernel,
        out_shape=[jax.ShapeDtypeStruct((rows, DET), F32) for rows in (FIRST, 2 * DET - FIRST + EXTRA)],
        in_specs=[pl.BlockSpec(memory_space=pltpu.SMEM)] * 3 + [vmem] * 4,
        out_specs=[vmem] * 2,
        compiler_params=pltpu.CompilerParams(vmem_limit_bytes=VMEM_LIMIT),
        name="sides",
        cost_estimate=pl.CostEstimate(flops=WEIGHT, bytes_accessed=WEIGHT // 400, transcendentals=0),
    )(here_at, left_at, above_at, *operands)


def merge_kernel(here_at, above_at, own_ref, left_ref, right_ref, below_ref, merged, down, up):
    left_row, left_col = corner_of(left_ref, 2 * DET)
    right_row, right_col = corner_of(right_ref, 2 * DET)
    _, below_col = corner_of(below_ref, 2 * DET - FIRST)
    above_col = above_at[0, 1].astype(F32)

    def strip(step, _):
        start = pl.multiple_of(step * STRIP, STRIP)
        row = lax.broadcasted_iota(jnp.int32, (STRIP, DET), 0) + start
        col = lax.broadcasted_iota(jnp.int32, (STRIP, DET), 1)
        for part in range(2):
            flat = pl.ds(pl.multiple_of(part * DET + start, STRIP), STRIP)
            values = merge_cells(
                row.astype(F32),
                col.astype(F32),
                (here_at[0, 0].astype(F32), here_at[0, 1].astype(F32)),
                (left_row, left_col),
                (right_row, right_col),
                (below_col, above_col),
                *(ref[flat, :] for ref in (own_ref, left_ref, right_ref)),
            )
            for ref, value in zip((merged, down, up), values):
                ref[part, pl.ds(start, STRIP), :] = value
        return 0

    lax.fori_loop(0, DET // STRIP, strip, 0, unroll=4)


def merge_call(here_at, above_at, *operands):
    vmem = pl.BlockSpec(memory_space=pltpu.VMEM)
    return pl.pallas_call(
        merge_kernel,
        out_shape=[jax.ShapeDtypeStruct((2, DET, DET), F32)] * 3,
        in_specs=[pl.BlockSpec(memory_space=pltpu.SMEM)] * 2 + [vmem] * 4,
        out_specs=[vmem] * 3,
        compiler_params=pltpu.CompilerParams(vmem_limit_bytes=VMEM_LIMIT),
        name="merge",
        cost_estimate=pl.CostEstimate(flops=WEIGHT, bytes_accessed=WEIGHT // 400, transcendentals=0),
    )(here_at, above_at, *operands)


def merge_cells(row, col, here_at, left_at, right_at, starts, own, left, right):
    below_start, above_start = starts
    inside = row < here_at[0]
    inside_left = row < left_at[0]
    inside_right = row < right_at[0]
    near = col >= here_at[1]
    left = jnp.where(col < left_at[1], left, 0.0)
    right = jnp.where(col >= right_at[1], right, 0.0)
    own_near = jnp.where(near, own, 0.0)
    own_far = jnp.where(near, 0.0, own)

    def gathered(wanted, start):
        kept = (lambda at, value: jnp.where(at, value, 0.0)) if wanted else (lambda at, value: jnp.where(at, 0.0, value))
        near_sum = kept(inside, own_near) + kept(inside_left, left)
        far_sum = kept(inside, own_far) + kept(inside_right, right)
        return jnp.where(col >= start, near_sum, far_sum)

    merged = own + jnp.where(
        near,
        jnp.where(inside ^ inside_left, 0.0, left),
        jnp.where(inside ^ inside_right, 0.0, right),
    )
    return merged, gathered(True, below_start), gathered(False, above_start)


def settle_cells(corners, row, col, own, left):
    here_at, left_at = corners
    own = jnp.where(col >= here_at[0, 1], own, 0.0)
    left = jnp.where(col < left_at[0, 1], left, 0.0)
    own_here, left_here = row >= here_at[0, 0], row >= left_at[0, 0]
    down = jnp.where(own_here, 0.0, own) + jnp.where(left_here, 0.0, left)
    stays = jnp.where(own_here, own, 0.0) + jnp.where(left_here, left, 0.0)
    return down, stays


def shifted(value, axis, steps):
    count = lax.axis_size(axis)
    initial, last = (max(0, -steps), min(count, count - steps))
    return lax.ppermute(value, axis, [(source, source + steps) for source in range(initial, last)])


def swapped(value, axis, distance):
    count = lax.axis_size(axis)
    return lax.ppermute(value, axis, [(source, source ^ distance) for source in range(count)])


def tile_parts(keep, send):
    count = lax.axis_size("tile")
    summed = keep + swapped(send, "frame", 1)
    return lax.all_to_all(summed.reshape(count, MODES * DET // count, DET), "tile", 0, 0)


def chip_sum(part):
    distance = 2
    while distance < lax.axis_size("frame"):
        part = part + swapped(part, "frame", distance)
        distance *= 2
    return part


def quick_chip_sum(part):
    if lax.axis_size("frame") != 16:
        return chip_sum(part)
    for pairs in (
        ((0, 1), (2, 3), (4, 5), (6, 7)),
        ((1, 2), (3, 4), (5, 6), (7, 0)),
        ((1, 6), (2, 5), (3, 0), (4, 7)),
    ):
        ways = [way for one, other in pairs for way in ((one, other), (other, one))]
        moves = [(2 * one + core, 2 * other + core) for one, other in ways for core in range(2)]
        part = part + lax.ppermute(part, "frame", moves)
    return part


def spread(part):
    count = lax.axis_size("tile")
    parts = jnp.broadcast_to(part[None], (count,) + part.shape)
    mine = lax.all_to_all(parts, "tile", 0, 0).reshape(MODES, DET, DET)
    return mine, swapped(mine, "frame", 1)


def per_device(object_field, probe_modes, measured, offsets, ramp_steps):
    tile_at, frame_at = lax.axis_index("tile"), lax.axis_index("frame")
    core = frame_at & 1
    place = jnp.stack(
        [
            core,
            (tile_at == lax.axis_size("tile") - 1).astype(jnp.int32),
            (frame_at == lax.axis_size("frame") - 1).astype(jnp.int32),
        ]
    )
    rate = probe_step / (lax.axis_size("tile") * lax.axis_size("frame"))
    together = lax.optimization_barrier

    flat = object_field.reshape(2 * DET, DET)
    first, second = flat[:FIRST], flat[FIRST:]
    lower = shifted(first, "tile", -1)
    right = shifted(second, "frame", -1)
    at_left = shifted(offsets, "frame", 1)
    at_above = shifted(offsets, "tile", 1)
    lower, right, at_left, at_above = together((lower, right, at_left, at_above))
    to_left, to_above = side_call(offsets, at_left, at_above, first, second, lower, right)
    side = shifted(to_left, "frame", -1)
    below = shifted(to_above, "tile", -1)

    ramp, _, _ = together((ramp_steps, to_left, to_above))
    vectors = jnp.asarray(shift_rows())
    side, below, *filled = together((side, below, *tables_call(ramp, vectors)))

    scalars = (offsets, ramp_steps, place)
    kept = (probe_modes, measured)
    grad1, patch, keep1, send1 = gradient_call(
        False, rate, scalars, (first, second, lower, right, side, below), kept + tuple(filled)
    )

    grad_left = shifted(grad1, "frame", 1)
    grad_right = shifted(grad1, "frame", -1)
    parts = tile_parts(keep1, send1)
    merged, down, up = merge_call(offsets, at_above, grad1, grad_left, grad_right, below)
    parts, _, _, _ = together((parts, merged, down, up))
    from_above = shifted(down, "tile", 1)
    from_below = shifted(up, "tile", -1)
    part = quick_chip_sum(jnp.sum(parts, axis=0))
    part, from_above, from_below = together((part, from_above, from_below))
    mine, other = spread(part)

    grad_total, keep2, send2, shift_grad = gradient_call(
        True,
        rate,
        scalars,
        (patch, merged, from_above, from_below, grad1, mine, other, keep1, send1),
        kept + (vectors,),
    )

    count = lax.axis_size("tile")
    planes = probe_modes.reshape(2, count, MODES * DET // count, DET)
    own_part = lax.dynamic_slice(planes, (core, tile_at, 0, 0), (1, 1) + planes.shape[2:])[0, 0]

    moved = shifted(grad_total, "frame", 1)
    parts = tile_parts(keep2, send2)
    down, stays = plane_call(
        "settle", settle_cells, (offsets, at_left), (grad_total, moved), 2, WEIGHT
    )
    parts, _, _ = together((parts, down, stays))
    part = jnp.sum(parts, axis=0)
    arrived = shifted(down, "tile", 1)
    part = own_part - rate * chip_sum(part)
    part, arrived = together((part, arrived))
    object_final = object_field - object_step * (stays + arrived)

    mine, other = spread(part)
    plane = lax.broadcasted_iota(jnp.int32, (2, MODES, DET, DET), 0)
    probe_final = jnp.where(plane == core, mine[None], other[None])
    return (object_final, probe_final, shift_grad)


def solution(mesh):
    placed = (
        P(None, "tile", "frame"),
        P(),
        P(("tile", "frame"), None, None),
        P(("tile", "frame"), None),
        P(("tile", "frame"), None),
    )
    return jax.shard_map(
        per_device,
        mesh=mesh,
        in_specs=placed,
        out_specs=(P(None, "tile", "frame"), P(), P(("tile", "frame"), None)),
        check_vma=False,
    )
```
